128 devices in a mesh: sq: 128 (over x, z, y, core).
Axes of the slice: x: 4, y: 4, z: 4, core: 2. Of those that a mesh axis runs over, the one named last changes fastest.
Arguments:
- tokens: bfloat16 [4096, 2880], P('sq'), may hold values from -6 to 6
- norm_gain: float32 [2880], replicated, may hold values from 0.25 to 1.75
- expert_ids: int32 [4096, 4], P('sq'), may hold values from 0 to 31, all different within a row; in each aligned block of 32 rows (0 to 31, 32 to 63, ...) at most 5 rows name the same one
- combine_weight: float32 [4096, 4], P('sq'), may hold values from 0.05 to 0.6
- cotangent: bfloat16 [4096, 2880], P('sq'), may hold values from -6 to 6
- w_gate: bfloat16 [128, 2880, 720], P('sq'), may hold values from -0.109375 to 0.109375
- w_up: bfloat16 [128, 2880, 720], P('sq'), may hold values from -0.109375 to 0.109375
- w_down: bfloat16 [128, 720, 2880], P('sq'), may hold values from -0.109375 to 0.109375
Outputs:
- d_tokens: bfloat16 [4096, 2880], P('sq')
- grad_gate: bfloat16 [128, 2880, 720], P('sq')
- grad_up: bfloat16 [128, 2880, 720], P('sq')
- grad_down: bfloat16 [128, 720, 2880], P('sq')
The draws below stay inside these ranges and needn't reach their ends.
Inputs may be any that keep to these rules, and one draw needn't show every extreme that they name: `expert_ids`: each row names 4 different experts; the rows of one device name any one expert at most 5 times, a bound that some block reaches.
All inputs are finite; a program needn't handle non-finite values.
Results may differ from the reference program's by a relative error of at most 0.0078.
Values may be sent and summed in bfloat16 or wider, within the bound.
A program may use at most 128 MiB of HBM per device.

```python
import math
import jax
import jax.numpy as jnp
import numpy as np
from jax import lax

D = 2880
FF = 2880
TOP = 4
QUARTERS = 4
TOK_DEV = 32
TOKENS = 4096
EXPERTS = 32
FF_Q = 720
SLOTS = 5
N_SQ = 128


def block_scale(stream_key, shape, pieces, least, top_value):
    level, own = 1.0, jax.random.fold_in(stream_key, 6)
    for dim, blocks in pieces:
        steps = jnp.exp(jax.random.uniform(jax.random.fold_in(own, dim), (blocks,), jnp.float32, least / len(pieces), top_value / len(pieces)))
        level = level * jnp.repeat(steps, shape[dim] // blocks).reshape([-1 if axis == dim else 1 for axis in range(len(shape))])
    return level


def routed_block(stream_key, own, number, rows, amount, top, bound, slope):
    sequence = jax.random.permutation(stream_key, amount)
    heavy_load, common = portions_of(amount, rows * top, bound, slope, True), portions_of(amount, rows * top, bound, slope, False)
    places = jnp.arange(amount)

    def named(lengths, offset_by):
        used = int((lengths > 0).sum())
        fixed = max(1, used // 4)
        moved = fixed + (places - fixed + offset_by * (used - fixed)) % max(1, amount - fixed)
        return jnp.zeros((amount,), jnp.int32).at[sequence[jnp.where(places < fixed, places, moved)]].set(jnp.asarray(lengths, jnp.int32))

    lengths = jnp.where(number % 4 == 0, named(heavy_load, number // 4), named(common, number - number // 4 - 1))
    mixed = jax.random.permutation(jax.random.fold_in(own, 3), amount)
    giver, receiver = mixed[0:amount // 2 * 2:2], mixed[1:amount // 2 * 2:2]
    slack = jnp.minimum(lengths[giver] - 1, bound - lengths[receiver]) // 2
    slack = jnp.where((giver == sequence[0]) | (receiver == sequence[0]) | (lengths[receiver] == 0), 0, jnp.maximum(slack, 0))
    moved = jax.random.randint(jax.random.fold_in(own, 4), (amount // 2,), 0, 1 << 20) % (slack + 1)
    lengths = lengths.at[giver].add(-moved).at[receiver].add(moved)
    items = jnp.searchsorted(jnp.cumsum(lengths), jnp.arange(rows * top), side="right").astype(jnp.int32)
    grid = items.reshape(top, rows).T
    grid = grid[jax.random.permutation(jax.random.fold_in(own, 1), rows)]
    offset_by = jax.random.randint(jax.random.fold_in(own, 2), (rows, 1), 0, top)
    return jnp.take_along_axis(grid, (jnp.arange(top)[None, :] + offset_by) % top, axis=1)


def portions_of(number_of, total, bound, lean, full):
    loads = [(1 << 20) // math.isqrt(rank ** lean) + 1 for rank in range(1, number_of + 1)]
    largest = bound if full else min(bound, max(-(-total // number_of), total * loads[0] // sum(loads)))
    least = 1 if total - largest >= number_of - 1 else 0
    holding, surplus = [largest] + [least] * (number_of - 1), total - largest - least * (number_of - 1)
    while surplus > 0:
        free = [i for i in range(1, number_of) if holding[i] < largest] or [i for i in range(1, number_of) if holding[i] < bound]
        pool, left = sum([loads[i] for i in free]), surplus
        for i in free:
            addition = min(bound - holding[i], max(1, left * loads[i] // pool), surplus)
            holding[i] = holding[i] + addition
            surplus = surplus - addition
    return np.array(holding)


def scatter_about(rng, extent, scale, reach, cuts=(), kind=jnp.bfloat16):
    values = jax.random.normal(rng, extent, jnp.float32) * scale
    if len(cuts) > 0:
        values = block_scale(rng, extent, cuts, -0.22, 0.18) * values
    return jnp.clip(values, min=-reach, max=reach).astype(kind)


def setup_inputs(seed: int = 0) -> dict:
    arg_keys = jax.random.split(jax.random.key(seed), 9)
    tokens = scatter_about(arg_keys[0], (TOKENS, D), 1.0, 6.0, ((0, 128),))
    norm_gain = jnp.clip(1.0 + 0.15 * jax.random.normal(arg_keys[1], (D,), jnp.float32), 0.25, 1.75)
    expert_ids_keys = jax.random.split(jax.random.fold_in(arg_keys[2], 1), TOKENS // TOK_DEV)
    expert_ids_turns = jax.random.permutation(jax.random.fold_in(arg_keys[2], 3), TOKENS // TOK_DEV)
    expert_ids = jax.vmap(lambda own, number: routed_block(jax.random.fold_in(arg_keys[2], 2), own, number, TOK_DEV, EXPERTS, TOP, SLOTS, 2))(expert_ids_keys, expert_ids_turns).reshape((TOKENS, TOP))
    combine_weight = jnp.clip(jnp.exp(math.log(0.6) - 2.4849067 * jax.random.uniform(arg_keys[3], (TOKENS, TOP), jnp.float32) ** block_scale(arg_keys[3], (TOKENS, TOP), ((0, 128),), -0.2, 0.2)), 0.05, 0.6)
    cotangent = scatter_about(arg_keys[4], (TOKENS, D), 1.0, 6.0, ((0, 128),))
    w_gate = scatter_about(arg_keys[5], (EXPERTS * QUARTERS, D, FF_Q), D ** -0.5, 0.109375, ((0, 128),))
    w_up = scatter_about(arg_keys[6], (EXPERTS * QUARTERS, D, FF_Q), D ** -0.5, 0.109375, ((0, 128),))
    w_down = scatter_about(arg_keys[7], (EXPERTS * QUARTERS, FF_Q, D), FF ** -0.5, 0.109375, ((0, 128),))
    return {"tokens": tokens, "norm_gain": norm_gain, "expert_ids": expert_ids, "combine_weight": combine_weight, "cotangent": cotangent, "w_gate": w_gate, "w_up": w_up, "w_down": w_down}


norm_eps = 1e-05
glu_alpha = 1.702

def expert_backward(x_in, dy_e, gate_w, up_w, down_w):
    gate = jnp.dot(x_in, gate_w, preferred_element_type=jnp.float32)
    up = jnp.dot(x_in, up_w, preferred_element_type=jnp.float32)
    sig = jax.nn.sigmoid(glu_alpha * gate)
    glu = gate * sig
    hid = (glu * (up + 1.0)).astype(jnp.bfloat16)
    d_hid = jnp.dot(dy_e, down_w.T, preferred_element_type=jnp.float32)
    d_up = (d_hid * glu).astype(jnp.bfloat16)
    d_gate = (d_hid * (up + 1.0) * (sig + glu_alpha * gate * sig * (1.0 - sig))).astype(jnp.bfloat16)
    partial_rows = jnp.dot(d_gate, gate_w.T, preferred_element_type=jnp.float32) + jnp.dot(d_up, up_w.T, preferred_element_type=jnp.float32)
    grad_g = jnp.dot(x_in.T, d_gate, preferred_element_type=jnp.float32).astype(jnp.bfloat16)
    grad_u = jnp.dot(x_in.T, d_up, preferred_element_type=jnp.float32).astype(jnp.bfloat16)
    grad_d = jnp.dot(hid.T, dy_e, preferred_element_type=jnp.float32).astype(jnp.bfloat16)
    return (partial_rows.astype(jnp.bfloat16), grad_g, grad_u, grad_d)

def reference(tokens, norm_gain, expert_ids, combine_weight, cotangent, w_gate, w_up, w_down):
    token_f = tokens.astype(jnp.float32)
    rstd = lax.rsqrt(lax.optimization_barrier(jnp.mean(token_f * token_f, axis=-1, keepdims=True)) + norm_eps)
    normed = (token_f * rstd * norm_gain).astype(jnp.bfloat16)
    picks = expert_ids.reshape(N_SQ, TOK_DEV * TOP)
    onehot = (picks[:, :, None] == jnp.arange(EXPERTS, dtype=jnp.int32)[None, None, :]).astype(jnp.int32)
    earlier = jnp.cumsum(onehot, axis=1) - onehot
    slot = lax.optimization_barrier(jnp.sum(earlier * onehot, axis=-1)).astype(jnp.int32)
    source = jnp.arange(N_SQ, dtype=jnp.int32)[:, None]
    position = (source * SLOTS + slot).reshape(-1).astype(jnp.int32)
    flat_expert = expert_ids.reshape(-1).astype(jnp.int32)
    pick_index = jnp.arange(TOKENS * TOP, dtype=jnp.int32)
    table = jnp.zeros((EXPERTS, N_SQ * SLOTS), jnp.int32).at[flat_expert, position].set(pick_index + 1)
    dy_pick = (combine_weight.reshape(-1)[:, None] * cotangent.astype(jnp.float32)[pick_index // TOP]).astype(jnp.bfloat16)

    def per_expert(inputs):
        entry, gate4, up4, down4 = inputs
        valid = (entry > 0)[:, None]
        which = jnp.maximum(entry - 1, 0).astype(jnp.int32)
        x_in = jnp.where(valid, normed[which // TOP], jnp.zeros((), jnp.bfloat16))
        dy_e = jnp.where(valid, dy_pick[which], jnp.zeros((), jnp.bfloat16))
        total = jnp.zeros((N_SQ * SLOTS, D), jnp.float32)
        grads_g, grads_u, grads_d = ([], [], [])
        for quarter in range(QUARTERS):
            part, grad_g, grad_u, grad_d = expert_backward(x_in, dy_e, gate4[quarter], up4[quarter], down4[quarter])
            total = total + part.astype(jnp.float32)
            grads_g.append(grad_g)
            grads_u.append(grad_u)
            grads_d.append(grad_d)
        return (total.astype(jnp.bfloat16), jnp.stack(grads_g), jnp.stack(grads_u), jnp.stack(grads_d))
    d_rows, grad_gate, grad_up, grad_down = lax.map(per_expert, (table, w_gate.reshape(EXPERTS, QUARTERS, D, FF_Q), w_up.reshape(EXPERTS, QUARTERS, D, FF_Q), w_down.reshape(EXPERTS, QUARTERS, FF_Q, D)))
    d_pick = d_rows[flat_expert, position].astype(jnp.float32)
    d_normed = lax.optimization_barrier(jnp.sum(d_pick.reshape(TOKENS, TOP, D), axis=1))
    scaled = d_normed * norm_gain
    mixed = lax.optimization_barrier(jnp.mean(token_f * scaled, axis=-1, keepdims=True))
    d_tokens = (rstd * scaled - token_f * rstd * rstd * rstd * mixed).astype(jnp.bfloat16)
    return (d_tokens, grad_gate.reshape(EXPERTS * QUARTERS, D, FF_Q), grad_up.reshape(EXPERTS * QUARTERS, D, FF_Q), grad_down.reshape(EXPERTS * QUARTERS, FF_Q, D))
```

```python
import functools

import jax
import jax.numpy as jnp
from jax import lax
from jax.experimental import pallas as pl
from jax.experimental.pallas import tpu as pltpu
from jax.sharding import PartitionSpec as P

MESH = pl.DeviceIdType.MESH
BF = jnp.bfloat16
F32 = jnp.float32

eps = 1e-05
alpha = 1.702

D = 2880
FQ = 720
TOK = 32
TOP = 4
SLOTS = 5
CW = 768
HW = CW // 2
NK = -(-D // CW)
VALID = [min(CW, D - k * CW) for k in range(NK)]
LANES = [-(-v // 128) * 128 for v in VALID]
EARLY = [False, False, False, False]
ROWS = 8 * SLOTS
BLK = 4 * ROWS
TOTAL = 4 * BLK
NG = 3
GB = FQ // NG


def dot(a, b):
    return jnp.dot(a, b, preferred_element_type=F32)


def dot_t(a, b):
    return lax.dot_general(a, b, (((1,), (1,)), ((), ())), preferred_element_type=F32)


def dot_0(a, b):
    return lax.dot_general(a, b, (((0,), (0,)), ((), ())), preferred_element_type=F32)


def device(x, z, y, c):
    return (((x * 4 + z) * 4 + y) * 2 + c,)


def kernel(
    tok_ref, gain_ref, ids_ref, cw_ref, cot_ref, wg_hbm, wu_hbm, wd_hbm,
    dtok_ref, gg_hbm, gu_hbm, gd_hbm,
    wg, wu, wd, own, meta_own, meta_got, gath, rows, xd, sel_f, sel, scale, up_a, gate_a, dhid_a,
    dg, du, dg_t, du_t, hid_t, part, part_got, psum, h_got, drow, z_got, tsum, x_got, f_out, f_got, dn, gs,
    wsem, psem, msem, msend, fsem, hsem, xsem, zsem, ysem, csem, rcsem, rhsem, rzsem, rxsem, rfsem,
    send, gsem,
):
    me = lax.axis_index("sq")
    c = lax.rem(me, 2)
    y = lax.rem(me // 2, 4)
    z = lax.rem(me // 8, 4)
    x = me // 32
    h = lax.rem(y, 2)
    half = y // 2
    yp = y + 1 - 2 * h
    yl = 3 - y
    any_early = any(EARLY)

    weights = [
        pltpu.make_async_copy(wg_hbm.at[0], wg, wsem.at[0]),
        pltpu.make_async_copy(wu_hbm.at[0], wu, wsem.at[1]),
        pltpu.make_async_copy(wd_hbm.at[0], wd, wsem.at[2]),
    ]
    for w in weights:
        w.start()

    peers_x = [(dx, dr) for dx in range(4) for dr in range(2) if (dx, dr) != (0, 0)]
    peers_z = [(dz, pr) for dz in range(4) for pr in range(2) if (dz, pr) != (0, 0)]

    def x_peer(dx, dr):
        return lax.rem(x + dx, 4), lax.rem(c + dr, 2)

    def z_peer(dz, pr):
        return lax.rem(z + dz, 4), (yl if pr else y)

    barrier = pltpu.get_barrier_semaphore()
    for p in peers_x:
        xx, cc = x_peer(*p)
        pl.semaphore_signal(barrier, inc=1, device_id=device(xx, z, y, cc), device_id_type=MESH)
    for p in peers_z:
        zz, yy = z_peer(*p)
        pl.semaphore_signal(barrier, inc=1, device_id=device(x, zz, yy, c), device_id_type=MESH)
    pl.semaphore_signal(barrier, inc=1, device_id=device(x, z, yp, c), device_id_type=MESH)

    def gain(lo, v):
        return gain_ref[pl.ds(lo, v)].reshape(1, v)

    tf = tok_ref[...].astype(F32)
    rstd = lax.rsqrt(jnp.mean(tf * tf, axis=-1, keepdims=True) + eps)
    for k in range(NK):
        lo, v, n = k * CW, VALID[k], LANES[k]
        if v < n:
            own[k, 0, h, :, :] = jnp.zeros((TOK, CW), BF)
            own[k, 1, h, :, :] = jnp.zeros((TOK, CW), BF)
        own[k, 0, h, :, 0:v] = (tf[:, lo : lo + v] * rstd * gain(lo, v)).astype(BF)
        own[k, 1, h, :, 0:v] = cot_ref[:, lo : lo + v]

    lane = lax.broadcasted_iota(jnp.int32, (TOK, 256), 1)
    trow = lax.broadcasted_iota(jnp.int32, (TOK, 256), 0)
    place = jnp.where(lane == trow + TOK * (2 * x + c), 1.0, 0.0).astype(BF)
    w_all = cw_ref[...]
    w_hi = w_all.astype(BF)
    w_rest = w_all - w_hi.astype(F32)
    w_mid = w_rest.astype(BF)
    w_lo = (w_rest - w_mid.astype(F32)).astype(BF)
    meta_own[h, 0:TOP, :] = dot(ids_ref[...].astype(F32).astype(BF), place)
    meta_own[h, TOP : 2 * TOP, :] = dot(w_hi, place) + dot(w_mid, place) + dot(w_lo, place)

    pl.semaphore_wait(barrier, len(peers_x) + len(peers_z) + 1)

    sends = []
    count = [0]

    def put(src, dst, recv, dev):
        cp = pltpu.make_async_remote_copy(
            src_ref=src, dst_ref=dst, send_sem=send.at[count[0]], recv_sem=recv,
            device_id=dev, device_id_type=MESH,
        )
        count[0] += 1
        cp.start()
        sends.append(cp)

    def arrived(dst, sem):
        pltpu.make_async_copy(dst, dst, sem).wait()

    src_mine = 2 * x + c

    for k in range(NK):
        if EARLY[k]:
            n = LANES[k]
            o = own.at[k, :, h, :, pl.ds(0, n)]
            put(o, o, fsem.at[k], device(x, z, yp, c))
    if any_early:
        put(meta_own.at[h], meta_own.at[h], fsem.at[NK], device(x, z, yp, c))

    def slabs(ref, index, row, count, n):
        return ref.at[(*index, pl.ds(row // 8, count // 8), slice(None), pl.ds(0, n))]

    def flat(ref, *index):
        r = ref.at[index]
        return r.reshape(r.shape[0] * 8, r.shape[2])

    def send_x(k):
        n = LANES[k]
        hs = [0, 1] if EARLY[k] else [h]
        if EARLY[k]:
            o = own.at[k, :, 1 - h, :, pl.ds(0, n)]
            arrived(o, fsem.at[k])
        for i, hh in enumerate(hs):
            for p in peers_x:
                xx, cc = x_peer(*p)
                put(
                    own.at[k, cc, hh, :, pl.ds(0, n)],
                    gath.at[k, hh, pl.ds(TOK * src_mine, TOK), pl.ds(0, n)],
                    xsem.at[k, i, src_mine],
                    device(xx, z, y, cc),
                )
            pltpu.make_async_copy(
                own.at[k, c, hh, :, pl.ds(0, n)],
                gath.at[k, hh, pl.ds(TOK * src_mine, TOK), pl.ds(0, n)],
                xsem.at[k, i, src_mine],
            ).start()

    hs_meta = [0, 1] if any_early else [h]

    def send_meta():
        if any_early:
            arrived(meta_own.at[1 - h], fsem.at[NK])
        for i, hh in enumerate(hs_meta):
            for p in peers_x:
                xx, cc = x_peer(*p)
                put(
                    meta_own.at[hh], meta_got.at[hh, src_mine], msem.at[i, src_mine],
                    device(xx, z, y, cc),
                )
            pltpu.make_async_copy(
                meta_own.at[hh], meta_got.at[hh, src_mine], msem.at[i, src_mine]
            ).start()

    late = [k for k in range(NK) if not EARLY[k]]
    order = list(range(NK))
    if not any_early:
        send_meta()
        for k in order:
            send_x(k)
    else:
        for k in late[:1]:
            send_x(k)
        send_meta()
        for k in order:
            if k not in late[:1]:
                send_x(k)

    def build():
        e_of = lax.broadcasted_iota(jnp.int32, (8, 256), 0).astype(F32) + (8 * x).astype(F32)
        t1 = lax.broadcasted_iota(jnp.int32, (256, 256), 0)
        t2 = lax.broadcasted_iota(jnp.int32, (256, 256), 1)
        lower = jnp.where((t1 < t2) & (t1 // TOK == t2 // TOK), 1.0, 0.0).astype(BF)
        r = lax.broadcasted_iota(jnp.int32, (ROWS, 256), 0)
        t = lax.broadcasted_iota(jnp.int32, (ROWS, 256), 1)
        src_ok = r // SLOTS == t // TOK
        slot_of = lax.rem(r, SLOTS).astype(F32)
        for i, hh in enumerate(hs_meta):
            for s in range(8):
                arrived(meta_got.at[hh, s], msem.at[i, s])
            meta = meta_got[hh, 0]
            for s in range(1, 8):
                meta = meta + meta_got[hh, s]
            named = jnp.zeros((8, 256), F32)
            weight = jnp.zeros((8, 256), F32)
            for j in range(TOP):
                hit = meta[j : j + 1, :] == e_of
                named = named + jnp.where(hit, 1.0, 0.0)
                weight = weight + jnp.where(hit, meta[TOP + j : TOP + j + 1, :], 0.0)
            rank = dot(named.astype(BF), lower)
            for e in range(8):
                on = src_ok & (rank[e : e + 1, :] == slot_of)
                one = jnp.where(on, jnp.broadcast_to(named[e : e + 1, :], (ROWS, 256)), 0.0)
                sel_f[pl.ds(e * ROWS, ROWS), :] = one
                w_row = jnp.sum(one * weight[e : e + 1, :], axis=-1, keepdims=True)
                scale[hh, pl.ds(e * ROWS, ROWS), :] = jnp.broadcast_to(
                    jnp.where(c == 0, jnp.ones_like(w_row), w_row), (ROWS, 128)
                )
            sel[hh, :, :] = sel_f[...].astype(BF)

    def select(k):
        n = LANES[k]
        hs = [0, 1] if EARLY[k] else [h]
        for i, hh in enumerate(hs):
            for s in range(8):
                arrived(gath.at[k, hh, pl.ds(TOK * s, TOK), pl.ds(0, n)], xsem.at[k, i, s])
        for i, hh in enumerate(hs):
            picked = dot(sel[hh], gath[k, hh, :, 0:n])
            picked = (picked * scale[hh, :, 0:1]).astype(BF)
            flat(rows, k, hh)[:, 0:n] = picked
            ys = 2 * half + hh if EARLY[k] else y
            for dz in range(4):
                for pr in range(2):
                    zz, yy = z_peer(dz, pr)
                    pp = half + pr * (1 - 2 * half)
                    src = slabs(rows, (k, hh), (zz * 2 + pp) * ROWS, ROWS, n)
                    dst = slabs(xd, (k, c), ys * BLK + z * ROWS, ROWS, n)
                    sem = zsem.at[k, i, pr, z]
                    if dz == 0 and pr == 0:
                        pltpu.make_async_copy(src, dst, sem).start()
                    else:
                        put(src, dst, sem, device(x, zz, yy, c))

    def block(k, ys):
        return slabs(xd, (k, c), ys * BLK, BLK, LANES[k])

    def wait_z(k, i, pr, ys):
        n = LANES[k]
        for s in range(4):
            arrived(slabs(xd, (k, c), ys * BLK + s * ROWS, ROWS, n), zsem.at[k, i, pr, s])

    def to_core(k, ys):
        put(block(k, ys), block(k, ys), csem.at[k, ys], device(x, z, y, 1 - c))

    def forward(k):
        if EARLY[k]:
            for pr in range(2):
                for i in range(2):
                    ys = 2 * (half + pr * (1 - 2 * half)) + i
                    wait_z(k, i, pr, ys)
                    to_core(k, ys)
        else:
            for pr, ys in enumerate((y, yl)):
                wait_z(k, 0, pr, ys)
                put(block(k, ys), block(k, ys), ysem.at[k, pr], device(x, z, yp, c))
                to_core(k, ys)

    def finish(k):
        if not EARLY[k]:
            for pr, ys in enumerate((yp, 3 - yp)):
                arrived(block(k, ys), ysem.at[k, pr])
                to_core(k, ys)

    def up_matmuls(k):
        n, v, lo = LANES[k], VALID[k], k * CW
        for ys in range(4):
            arrived(slabs(xd, (k, 1 - c), ys * BLK, BLK, n), csem.at[k, ys])
        if k == 0:
            for w in weights:
                w.wait()
        xs = flat(xd, k, 0)[:, 0:v]
        gate = dot_t(xs, wg[:, lo : lo + v])
        gate_a[...] = gate if k == 0 else gate_a[...] + gate
        up = dot_t(xs, wu[:, lo : lo + v])
        up_a[...] = up if k == 0 else up_a[...] + up
        dhid = dot_t(flat(xd, k, 1)[:, 0:v], wd[:, lo : lo + v])
        dhid_a[...] = dhid if k == 0 else dhid_a[...] + dhid

    build()
    for step in range(NK + 3):
        if step < NK:
            select(step)
        if 0 <= step - 1 < NK:
            forward(step - 1)
        if 0 <= step - 2 < NK:
            finish(step - 2)
        if 0 <= step - 3 < NK:
            up_matmuls(step - 3)

    def pointwise(i, carry):
        b = pl.ds(pl.multiple_of(i * BLK, BLK), BLK)
        gate = gate_a[b, :]
        sig = jax.nn.sigmoid(alpha * gate)
        glu = gate * sig
        up1 = up_a[b, :] + 1.0
        gate_a[b, :] = glu * up1
        d_hid = dhid_a[b, :]
        du[b, :] = (d_hid * glu).astype(BF)
        dg[b, :] = (d_hid * up1 * (sig + alpha * gate * sig * (1.0 - sig))).astype(BF)
        return carry

    lax.fori_loop(0, 4, pointwise, 0)

    def partial(k):
        lo, v = k * CW, VALID[k]
        if v < CW:
            part[k, 1, :, :] = jnp.zeros((TOTAL, HW), BF)
        p = dot(dg[...], wg[:, lo : lo + v]) + dot(du[...], wu[:, lo : lo + v])
        p = p.astype(BF)
        part[k, 0, :, :] = p[:, 0:HW]
        part[k, 1, :, 0 : v - HW] = p[:, HW:v]
        put(part.at[k, 1 - c], part_got.at[k], rcsem.at[k], device(x, z, y, 1 - c))

    def back_z(k, src_ref, base_of):
        for pr in range(2):
            ydst = yl if pr else y
            his = [0, 1] if EARLY[k] else [0]
            for i in his:
                hd = i if EARLY[k] else lax.rem(ydst, 2)
                for dz in range(4):
                    zz = lax.rem(z + dz, 4)
                    src = slabs(src_ref, (k,), base_of(pr, i) * BLK + zz * ROWS, ROWS, HW)
                    dst = slabs(z_got, (k, hd), (z * 2 + half) * ROWS, ROWS, HW)
                    sem = rzsem.at[k, i, z * 2 + half]
                    if dz == 0 and pr == 0:
                        pltpu.make_async_copy(src, dst, sem).start()
                    else:
                        put(src, dst, sem, device(x, zz, ydst, c))

    def back_core(k):
        arrived(part_got.at[k], rcsem.at[k])
        flat(psum, k)[...] = (part[k, c].astype(F32) + part_got[k].astype(F32)).astype(BF)
        if EARLY[k]:
            back_z(k, psum, lambda pr, i: 2 * (half + pr * (1 - 2 * half)) + i)
        else:
            for j, ys in enumerate((yp, 3 - yp)):
                put(
                    slabs(psum, (k,), ys * BLK, BLK, HW), slabs(h_got, (k,), j * BLK, BLK, HW),
                    rhsem.at[k, j], device(x, z, yp, c),
                )

    def back_pair(k):
        if not EARLY[k]:
            for j, ys in enumerate((y, yl)):
                arrived(slabs(h_got, (k,), j * BLK, BLK, HW), rhsem.at[k, j])
                b = pl.ds(pl.multiple_of(ys * BLK, BLK), BLK)
                to = pl.ds(j * BLK, BLK)
                flat(drow, k)[to, :] = (
                    flat(psum, k)[b, :].astype(F32) + flat(h_got, k)[to, :].astype(F32)
                ).astype(BF)
            back_z(k, drow, lambda pr, i: pr)

    def back_token(k):
        hs = [0, 1] if EARLY[k] else [h]
        for i, hh in enumerate(hs):
            for e in range(8):
                arrived(slabs(z_got, (k, hh), e * ROWS, ROWS, HW), rzsem.at[k, i, e])
        for i, hh in enumerate(hs):
            tsum[k, hh, :, :] = dot_0(sel[hh], flat(z_got, k, hh)[...]).astype(BF)
            for p in peers_x:
                xx, cc = x_peer(*p)
                put(
                    tsum.at[k, hh, pl.ds((2 * xx + cc) * TOK, TOK), :],
                    x_got.at[k, hh, src_mine],
                    rxsem.at[k, i, src_mine],
                    device(xx, z, y, cc),
                )
            pltpu.make_async_copy(
                tsum.at[k, hh, pl.ds(src_mine * TOK, TOK), :],
                x_got.at[k, hh, src_mine],
                rxsem.at[k, i, src_mine],
            ).start()

    def gather_sum(k, hh, r):
        s = x_got[k, hh, r].astype(F32)
        for j in range(1, 4):
            s = s + x_got[k, hh, 2 * j + r].astype(F32)
        return s

    def back_x(k):
        hs = [0, 1] if EARLY[k] else [h]
        for i, hh in enumerate(hs):
            for s in range(8):
                arrived(x_got.at[k, hh, s], rxsem.at[k, i, s])
        for r in range(2):
            dn[2 * k + r] = gather_sum(k, h, r)
        if EARLY[k]:
            for r in range(2):
                f_out[k, r] = gather_sum(k, 1 - h, r).astype(BF)
            put(f_out.at[k], f_got.at[k], rfsem.at[k], device(x, z, yp, c))

    def back_last(k):
        if EARLY[k]:
            arrived(f_got.at[k], rfsem.at[k])
            for r in range(2):
                dn[2 * k + r] = dn[2 * k + r] + f_got[k, r].astype(F32)

    stores = []

    def grad(which, b):
        slot = len(stores) % 2
        if len(stores) >= 2:
            stores[-2].wait()
        left = (dg_t, du_t, hid_t)[which]
        for k in range(NK):
            lo, v = k * CW, VALID[k]
            gs[slot, :, lo : lo + v] = dot(
                left[b * GB : (b + 1) * GB, :], flat(xd, k, which // 2)[:, 0:v]
            ).astype(BF)
        cp = pltpu.make_async_copy(
            gs.at[slot], (gg_hbm, gu_hbm, gd_hbm)[which].at[0, pl.ds(b * GB, GB), :],
            gsem.at[len(stores)],
        )
        cp.start()
        stores.append(cp)

    fill = [lambda w=w, b=b: grad(w, b) for w in range(3) for b in range(NG)]

    def filler():
        if fill:
            fill.pop(0)()

    for step in range(NK + 5):
        if step < NK:
            partial(step)
        if step == 0:
            hid_t[...] = gate_a[...].T.astype(BF)
            dg_t[...] = dg[...].T
            du_t[...] = du[...].T
        if 0 <= step - 1 < NK:
            back_core(step - 1)
        if 0 <= step - 2 < NK:
            back_pair(step - 2)
        if step >= 2:
            filler()
        if 0 <= step - 3 < NK:
            back_token(step - 3)
        if 0 <= step - 4 < NK:
            back_x(step - 4)
        if 0 <= step - 5 < NK:
            back_last(step - 5)
    while fill:
        filler()

    total = jnp.zeros((TOK, 1), F32)
    for k in range(NK):
        for r in range(2):
            lo = k * CW + r * HW
            v = max(0, min(HW, D - lo))
            if v:
                u = dn[2 * k + r, :, 0:v] * gain(lo, v)
                dn[2 * k + r, :, 0:v] = u
                total = total + jnp.sum(tf[:, lo : lo + v] * u, axis=-1, keepdims=True)
    mixed = rstd * rstd * rstd * (total / D)
    for k in range(NK):
        for r in range(2):
            lo = k * CW + r * HW
            v = max(0, min(HW, D - lo))
            if v:
                dtok_ref[:, lo : lo + v] = (
                    rstd * dn[2 * k + r, :, 0:v] - tf[:, lo : lo + v] * mixed
                ).astype(BF)

    for cp in stores[-2:]:
        cp.wait()
    for cp in sends:
        cp.wait_send()


def n_sends():
    early = sum(EARLY)
    late = NK - early
    n = early + (1 if early else 0)
    n += 7 * (late + 2 * early) + 7 * (2 if early else 1)
    n += 7 * (late + 2 * early) + 2 * late + 4 * NK
    n += NK + 2 * late + 7 * (late + 2 * early) + 7 * (late + 2 * early) + early
    return n


def local(tokens, norm_gain, expert_ids, combine_weight, cotangent, w_gate, w_up, w_down):
    vm = pl.BlockSpec(memory_space=pltpu.VMEM)
    hbm = pl.BlockSpec(memory_space=pl.ANY)
    dma = pltpu.SemaphoreType.DMA
    scratch = [
        pltpu.VMEM((FQ, D), BF), pltpu.VMEM((FQ, D), BF), pltpu.VMEM((FQ, D), BF),
        pltpu.VMEM((NK, 2, 2, TOK, CW), BF),
        pltpu.VMEM((2, 8, 256), F32), pltpu.VMEM((2, 8, 8, 256), F32),
        pltpu.VMEM((NK, 2, 256, CW), BF),
        pltpu.VMEM((NK, 2, ROWS, 8, CW), BF),
        pltpu.VMEM((NK, 2, TOTAL // 8, 8, CW), BF),
        pltpu.VMEM((8 * ROWS, 256), F32), pltpu.VMEM((2, 8 * ROWS, 256), BF),
        pltpu.VMEM((2, 8 * ROWS, 128), F32),
        pltpu.VMEM((TOTAL, FQ), F32), pltpu.VMEM((TOTAL, FQ), F32), pltpu.VMEM((TOTAL, FQ), F32),
        pltpu.VMEM((TOTAL, FQ), BF), pltpu.VMEM((TOTAL, FQ), BF),
        pltpu.VMEM((FQ, TOTAL), BF), pltpu.VMEM((FQ, TOTAL), BF), pltpu.VMEM((FQ, TOTAL), BF),
        pltpu.VMEM((NK, 2, TOTAL, HW), BF),
        pltpu.VMEM((NK, TOTAL, HW), BF),
        pltpu.VMEM((NK, TOTAL // 8, 8, HW), BF),
        pltpu.VMEM((NK, BLK // 4, 8, HW), BF), pltpu.VMEM((NK, BLK // 4, 8, HW), BF),
        pltpu.VMEM((NK, 2, ROWS, 8, HW), BF), pltpu.VMEM((NK, 2, 256, HW), BF),
        pltpu.VMEM((NK, 2, 8, TOK, HW), BF),
        pltpu.VMEM((NK, 2, TOK, HW), BF), pltpu.VMEM((NK, 2, TOK, HW), BF),
        pltpu.VMEM((2 * NK, TOK, HW), F32),
        pltpu.VMEM((2, GB, D), BF),
        dma((3,)), dma((1,)), dma((2, 8)), dma((1,)), dma((NK + 1,)), dma((1,)), dma((NK, 2, 8)),
        dma((NK, 2, 2, 4)), dma((NK, 2)), dma((NK, 4)), dma((NK,)), dma((NK, 2)), dma((NK, 2, 8)),
        dma((NK, 2, 8)), dma((NK,)), dma((n_sends(),)), dma((3 * NG,)),
    ]
    d_tokens, grad_gate, grad_up, grad_down = pl.pallas_call(
        kernel,
        out_shape=(
            jax.ShapeDtypeStruct((TOK, D), BF),
            jax.ShapeDtypeStruct((1, FQ, D), BF),
            jax.ShapeDtypeStruct((1, FQ, D), BF),
            jax.ShapeDtypeStruct((1, FQ, D), BF),
        ),
        in_specs=[vm, vm, vm, vm, vm, hbm, hbm, hbm],
        out_specs=(vm, hbm, hbm, hbm),
        scratch_shapes=scratch,
        compiler_params=pltpu.CompilerParams(
            collective_id=0, has_side_effects=True, vmem_limit_bytes=63 << 20
        ),
    )(
        tokens, norm_gain, expert_ids.T, combine_weight.T, cotangent,
        jnp.swapaxes(w_gate, 1, 2), jnp.swapaxes(w_up, 1, 2), w_down,
    )
    return d_tokens, jnp.swapaxes(grad_gate, 1, 2), jnp.swapaxes(grad_up, 1, 2), grad_down


def solution(mesh):
    placed = (
        P("sq", None),
        P(),
        P("sq", None),
        P("sq", None),
        P("sq", None),
        P("sq", None, None),
        P("sq", None, None),
        P("sq", None, None),
    )
    return jax.shard_map(
        local,
        mesh=mesh,
        in_specs=placed,
        out_specs=(P("sq", None), P("sq", None, None), P("sq", None, None), P("sq", None, None)),
        check_vma=False,
    )
```

```python
import functools

import jax
import jax.numpy as jnp
from jax import lax
from jax.experimental import pallas as pl
from jax.experimental.pallas import tpu as pltpu
from jax.sharding import PartitionSpec as P

MESH = pl.DeviceIdType.MESH
BF = jnp.bfloat16
F32 = jnp.float32

eps = 1e-05
alpha = 1.702

D = 2880
FQ = 720
TOK = 32
TOP = 4
SLOTS = 5
CW = 512
HW = CW // 2
NK = -(-D // CW)
VALID = [min(CW, D - k * CW) for k in range(NK)]
LANES = [-(-v // 128) * 128 for v in VALID]
EARLY = [False, False, False, True, True, False]
WINDOW = 2
ROWS = 8 * SLOTS
BLK = 4 * ROWS
TOTAL = 4 * BLK
NG = 3
GB = FQ // NG


def dot(a, b):
    return jnp.dot(a, b, preferred_element_type=F32)


def dot_t(a, b):
    return lax.dot_general(a, b, (((1,), (1,)), ((), ())), preferred_element_type=F32)


def dot_0(a, b):
    return lax.dot_general(a, b, (((0,), (0,)), ((), ())), preferred_element_type=F32)


def device(x, z, y, c):
    return (((x * 4 + z) * 4 + y) * 2 + c,)


def kernel(
    tok_ref, gain_ref, ids_ref, cw_ref, cot_ref, wg_hbm, wu_hbm, wd_hbm,
    dtok_ref, gg_ref, gu_ref, gd_ref,
    own, meta_own, meta_got, gath, rows, xd, sel_f, sel, scale, up_a, gate_a, dhid_a,
    dg, du, dg_t, du_t, hid_t, part, part_got, psum, h_got, drow, z_got, tsum, x_got, f_out, f_got, dn,
    wsem, psem, msem, msend, fsem, hsem, xsem, zsem, ysem, csem, rcsem, rhsem, rzsem, rxsem, rfsem,
    send,
):
    me = lax.axis_index("sq")
    c = lax.rem(me, 2)
    y = lax.rem(me // 2, 4)
    z = lax.rem(me // 8, 4)
    x = me // 32
    h = lax.rem(y, 2)
    half = y // 2
    yp = y + 1 - 2 * h
    yl = 3 - y
    any_early = any(EARLY)

    wg, wu, wd = gg_ref.at[0], gu_ref.at[0], gd_ref.at[0]
    weights = [
        pltpu.make_async_copy(wg_hbm.at[0], wg, wsem.at[0]),
        pltpu.make_async_copy(wu_hbm.at[0], wu, wsem.at[1]),
        pltpu.make_async_copy(wd_hbm.at[0], wd, wsem.at[2]),
    ]
    for w in weights:
        w.start()

    peers_x = [(dx, dr) for dx in range(4) for dr in range(2) if (dx, dr) != (0, 0)]
    peers_z = [(dz, pr) for dz in range(4) for pr in range(2) if (dz, pr) != (0, 0)]

    def x_peer(dx, dr):
        return lax.rem(x + dx, 4), lax.rem(c + dr, 2)

    def z_peer(dz, pr):
        return lax.rem(z + dz, 4), (yl if pr else y)

    barrier = pltpu.get_barrier_semaphore()
    for p in peers_x:
        xx, cc = x_peer(*p)
        pl.semaphore_signal(barrier, inc=1, device_id=device(xx, z, y, cc), device_id_type=MESH)
    for p in peers_z:
        zz, yy = z_peer(*p)
        pl.semaphore_signal(barrier, inc=1, device_id=device(x, zz, yy, c), device_id_type=MESH)
    pl.semaphore_signal(barrier, inc=1, device_id=device(x, z, yp, c), device_id_type=MESH)

    def gain(lo, v):
        return gain_ref[pl.ds(lo, v)].reshape(1, v)

    tf = tok_ref[...].astype(F32)
    rstd = lax.rsqrt(jnp.mean(tf * tf, axis=-1, keepdims=True) + eps)
    for k in range(NK):
        lo, v, n = k * CW, VALID[k], LANES[k]
        if v < n:
            own[k, 0, h, :, :] = jnp.zeros((TOK, CW), BF)
            own[k, 1, h, :, :] = jnp.zeros((TOK, CW), BF)
        own[k, 0, h, :, 0:v] = (tf[:, lo : lo + v] * rstd * gain(lo, v)).astype(BF)
        own[k, 1, h, :, 0:v] = cot_ref[:, lo : lo + v]

    lane = lax.broadcasted_iota(jnp.int32, (TOK, 256), 1)
    trow = lax.broadcasted_iota(jnp.int32, (TOK, 256), 0)
    place = jnp.where(lane == trow + TOK * (2 * x + c), 1.0, 0.0).astype(BF)
    w_all = cw_ref[...]
    w_hi = w_all.astype(BF)
    w_rest = w_all - w_hi.astype(F32)
    w_mid = w_rest.astype(BF)
    w_lo = (w_rest - w_mid.astype(F32)).astype(BF)
    meta_own[h, 0:TOP, :] = dot(ids_ref[...].astype(F32).astype(BF), place)
    meta_own[h, TOP : 2 * TOP, :] = dot(w_hi, place) + dot(w_mid, place) + dot(w_lo, place)

    pl.semaphore_wait(barrier, len(peers_x) + len(peers_z) + 1)

    sends = []
    count = [0]

    def put(src, dst, recv, dev):
        cp = pltpu.make_async_remote_copy(
            src_ref=src, dst_ref=dst, send_sem=send.at[count[0]], recv_sem=recv,
            device_id=dev, device_id_type=MESH,
        )
        count[0] += 1
        cp.start()
        sends.append(cp)

    def arrived(dst, sem):
        pltpu.make_async_copy(dst, dst, sem).wait()

    src_mine = 2 * x + c

    for k in range(NK):
        if EARLY[k]:
            n = LANES[k]
            o = own.at[k, :, h, :, pl.ds(0, n)]
            put(o, o, fsem.at[k], device(x, z, yp, c))
    if any_early:
        put(meta_own.at[h], meta_own.at[h], fsem.at[NK], device(x, z, yp, c))

    def slabs(ref, index, row, count, n):
        return ref.at[(*index, pl.ds(row // 8, count // 8), slice(None), pl.ds(0, n))]

    def flat(ref, *index):
        r = ref.at[index]
        return r.reshape(r.shape[0] * 8, r.shape[2])

    def send_x(k):
        n = LANES[k]
        hs = [0, 1] if EARLY[k] else [h]
        if EARLY[k]:
            o = own.at[k, :, 1 - h, :, pl.ds(0, n)]
            arrived(o, fsem.at[k])
        for i, hh in enumerate(hs):
            for p in peers_x:
                xx, cc = x_peer(*p)
                put(
                    own.at[k, cc, hh, :, pl.ds(0, n)],
                    gath.at[k, hh, pl.ds(TOK * src_mine, TOK), pl.ds(0, n)],
                    xsem.at[k, i, src_mine],
                    device(xx, z, y, cc),
                )
            pltpu.make_async_copy(
                own.at[k, c, hh, :, pl.ds(0, n)],
                gath.at[k, hh, pl.ds(TOK * src_mine, TOK), pl.ds(0, n)],
                xsem.at[k, i, src_mine],
            ).start()

    hs_meta = [0, 1] if any_early else [h]

    def send_meta():
        if any_early:
            arrived(meta_own.at[1 - h], fsem.at[NK])
        for i, hh in enumerate(hs_meta):
            for p in peers_x:
                xx, cc = x_peer(*p)
                put(
                    meta_own.at[hh], meta_got.at[hh, src_mine], msem.at[i, src_mine],
                    device(xx, z, y, cc),
                )
            pltpu.make_async_copy(
                meta_own.at[hh], meta_got.at[hh, src_mine], msem.at[i, src_mine]
            ).start()

    if EARLY[0] or not any_early:
        send_meta()
        send_x(0)
    else:
        send_x(0)
        send_meta()
    for k in range(1, WINDOW):
        send_x(k)

    def build():
        e_of = lax.broadcasted_iota(jnp.int32, (8, 256), 0).astype(F32) + (8 * x).astype(F32)
        t1 = lax.broadcasted_iota(jnp.int32, (256, 256), 0)
        t2 = lax.broadcasted_iota(jnp.int32, (256, 256), 1)
        lower = jnp.where((t1 < t2) & (t1 // TOK == t2 // TOK), 1.0, 0.0).astype(BF)
        r = lax.broadcasted_iota(jnp.int32, (ROWS, 256), 0)
        t = lax.broadcasted_iota(jnp.int32, (ROWS, 256), 1)
        src_ok = r // SLOTS == t // TOK
        slot_of = lax.rem(r, SLOTS).astype(F32)
        for i, hh in enumerate(hs_meta):
            for s in range(8):
                arrived(meta_got.at[hh, s], msem.at[i, s])
            meta = meta_got[hh, 0]
            for s in range(1, 8):
                meta = meta + meta_got[hh, s]
            named = jnp.zeros((8, 256), F32)
            weight = jnp.zeros((8, 256), F32)
            for j in range(TOP):
                hit = meta[j : j + 1, :] == e_of
                named = named + jnp.where(hit, 1.0, 0.0)
                weight = weight + jnp.where(hit, meta[TOP + j : TOP + j + 1, :], 0.0)
            rank = dot(named.astype(BF), lower)
            for e in range(8):
                on = src_ok & (rank[e : e + 1, :] == slot_of)
                one = jnp.where(on, jnp.broadcast_to(named[e : e + 1, :], (ROWS, 256)), 0.0)
                sel_f[pl.ds(e * ROWS, ROWS), :] = one
                w_row = jnp.sum(one * weight[e : e + 1, :], axis=-1, keepdims=True)
                scale[hh, pl.ds(e * ROWS, ROWS), :] = jnp.broadcast_to(
                    jnp.where(c == 0, jnp.ones_like(w_row), w_row), (ROWS, 128)
                )
            sel[hh, :, :] = sel_f[...].astype(BF)

    def select(k):
        n = LANES[k]
        hs = [0, 1] if EARLY[k] else [h]
        for i, hh in enumerate(hs):
            for s in range(8):
                arrived(gath.at[k, hh, pl.ds(TOK * s, TOK), pl.ds(0, n)], xsem.at[k, i, s])
        if k + WINDOW < NK:
            send_x(k + WINDOW)
        for i, hh in enumerate(hs):
            picked = dot(sel[hh], gath[k, hh, :, 0:n])
            picked = (picked * scale[hh, :, 0:1]).astype(BF)
            flat(rows, k, hh)[:, 0:n] = picked
            ys = 2 * half + hh if EARLY[k] else y
            for dz in range(4):
                for pr in range(2):
                    zz, yy = z_peer(dz, pr)
                    pp = half + pr * (1 - 2 * half)
                    src = slabs(rows, (k, hh), (zz * 2 + pp) * ROWS, ROWS, n)
                    dst = slabs(xd, (k, c), ys * BLK + z * ROWS, ROWS, n)
                    sem = zsem.at[k, i, pr, z]
                    if dz == 0 and pr == 0:
                        pltpu.make_async_copy(src, dst, sem).start()
                    else:
                        put(src, dst, sem, device(x, zz, yy, c))

    def block(k, ys):
        return slabs(xd, (k, c), ys * BLK, BLK, LANES[k])

    def wait_z(k, i, pr, ys):
        n = LANES[k]
        for s in range(4):
            arrived(slabs(xd, (k, c), ys * BLK + s * ROWS, ROWS, n), zsem.at[k, i, pr, s])

    def to_core(k, ys):
        put(block(k, ys), block(k, ys), csem.at[k, ys], device(x, z, y, 1 - c))

    def forward(k):
        if EARLY[k]:
            for pr in range(2):
                for i in range(2):
                    ys = 2 * (half + pr * (1 - 2 * half)) + i
                    wait_z(k, i, pr, ys)
                    to_core(k, ys)
        else:
            for pr, ys in enumerate((y, yl)):
                wait_z(k, 0, pr, ys)
                put(block(k, ys), block(k, ys), ysem.at[k, pr], device(x, z, yp, c))
                to_core(k, ys)

    def finish(k):
        if not EARLY[k]:
            for pr, ys in enumerate((yp, 3 - yp)):
                arrived(block(k, ys), ysem.at[k, pr])
                to_core(k, ys)

    def up_matmuls(k):
        n, v, lo = LANES[k], VALID[k], k * CW
        for ys in range(4):
            arrived(slabs(xd, (k, 1 - c), ys * BLK, BLK, n), csem.at[k, ys])
        if k == 0:
            for w in weights:
                w.wait()
        xs = flat(xd, k, 0)[:, 0:v]
        gate = dot_t(xs, wg[:, lo : lo + v])
        gate_a[...] = gate if k == 0 else gate_a[...] + gate
        up = dot_t(xs, wu[:, lo : lo + v])
        up_a[...] = up if k == 0 else up_a[...] + up
        dhid = dot_t(flat(xd, k, 1)[:, 0:v], wd[:, lo : lo + v])
        dhid_a[...] = dhid if k == 0 else dhid_a[...] + dhid

    build()
    for step in range(NK + 3):
        if step < NK:
            select(step)
        if 0 <= step - 1 < NK:
            forward(step - 1)
        if 0 <= step - 2 < NK:
            finish(step - 2)
        if 0 <= step - 3 < NK:
            up_matmuls(step - 3)

    def pointwise(i, carry):
        b = pl.ds(pl.multiple_of(i * BLK, BLK), BLK)
        gate = gate_a[b, :]
        sig = jax.nn.sigmoid(alpha * gate)
        glu = gate * sig
        up1 = up_a[b, :] + 1.0
        gate_a[b, :] = glu * up1
        d_hid = dhid_a[b, :]
        du[b, :] = (d_hid * glu).astype(BF)
        dg[b, :] = (d_hid * up1 * (sig + alpha * gate * sig * (1.0 - sig))).astype(BF)
        return carry

    lax.fori_loop(0, 4, pointwise, 0)

    def partial(k):
        lo, v = k * CW, VALID[k]
        if v < CW:
            part[k, 1, :, :] = jnp.zeros((TOTAL, HW), BF)
        p = dot(dg[...], wg[:, lo : lo + v]) + dot(du[...], wu[:, lo : lo + v])
        p = p.astype(BF)
        part[k, 0, :, :] = p[:, 0:HW]
        part[k, 1, :, 0 : v - HW] = p[:, HW:v]
        put(part.at[k, 1 - c], part_got.at[k], rcsem.at[k], device(x, z, y, 1 - c))

    def back_z(k, src_ref, base_of):
        for pr in range(2):
            ydst = yl if pr else y
            his = [0, 1] if EARLY[k] else [0]
            for i in his:
                hd = i if EARLY[k] else lax.rem(ydst, 2)
                for dz in range(4):
                    zz = lax.rem(z + dz, 4)
                    src = slabs(src_ref, (k,), base_of(pr, i) * BLK + zz * ROWS, ROWS, HW)
                    dst = slabs(z_got, (k, hd), (z * 2 + half) * ROWS, ROWS, HW)
                    sem = rzsem.at[k, i, z * 2 + half]
                    if dz == 0 and pr == 0:
                        pltpu.make_async_copy(src, dst, sem).start()
                    else:
                        put(src, dst, sem, device(x, zz, ydst, c))

    def back_core(k):
        arrived(part_got.at[k], rcsem.at[k])
        flat(psum, k)[...] = (part[k, c].astype(F32) + part_got[k].astype(F32)).astype(BF)
        if EARLY[k]:
            back_z(k, psum, lambda pr, i: 2 * (half + pr * (1 - 2 * half)) + i)
        else:
            for j, ys in enumerate((yp, 3 - yp)):
                put(
                    slabs(psum, (k,), ys * BLK, BLK, HW), slabs(h_got, (k,), j * BLK, BLK, HW),
                    rhsem.at[k, j], device(x, z, yp, c),
                )

    def back_pair(k):
        if not EARLY[k]:
            for j, ys in enumerate((y, yl)):
                arrived(slabs(h_got, (k,), j * BLK, BLK, HW), rhsem.at[k, j])
                b = pl.ds(pl.multiple_of(ys * BLK, BLK), BLK)
                to = pl.ds(j * BLK, BLK)
                flat(drow, k)[to, :] = (
                    flat(psum, k)[b, :].astype(F32) + flat(h_got, k)[to, :].astype(F32)
                ).astype(BF)
            back_z(k, drow, lambda pr, i: pr)

    def back_token(k):
        hs = [0, 1] if EARLY[k] else [h]
        for i, hh in enumerate(hs):
            for e in range(8):
                arrived(slabs(z_got, (k, hh), e * ROWS, ROWS, HW), rzsem.at[k, i, e])
        for i, hh in enumerate(hs):
            tsum[k, hh, :, :] = dot_0(sel[hh], flat(z_got, k, hh)[...]).astype(BF)
            for p in peers_x:
                xx, cc = x_peer(*p)
                put(
                    tsum.at[k, hh, pl.ds((2 * xx + cc) * TOK, TOK), :],
                    x_got.at[k, hh, src_mine],
                    rxsem.at[k, i, src_mine],
                    device(xx, z, y, cc),
                )
            pltpu.make_async_copy(
                tsum.at[k, hh, pl.ds(src_mine * TOK, TOK), :],
                x_got.at[k, hh, src_mine],
                rxsem.at[k, i, src_mine],
            ).start()

    def gather_sum(k, hh, r):
        s = x_got[k, hh, r].astype(F32)
        for j in range(1, 4):
            s = s + x_got[k, hh, 2 * j + r].astype(F32)
        return s

    def back_x(k):
        hs = [0, 1] if EARLY[k] else [h]
        for i, hh in enumerate(hs):
            for s in range(8):
                arrived(x_got.at[k, hh, s], rxsem.at[k, i, s])
        for r in range(2):
            dn[2 * k + r] = gather_sum(k, h, r)
        if EARLY[k]:
            for r in range(2):
                f_out[k, r] = gather_sum(k, 1 - h, r).astype(BF)
            put(f_out.at[k], f_got.at[k], rfsem.at[k], device(x, z, yp, c))

    def back_last(k):
        if EARLY[k]:
            arrived(f_got.at[k], rfsem.at[k])
            for r in range(2):
                dn[2 * k + r] = dn[2 * k + r] + f_got[k, r].astype(F32)

    def grad(which, b):
        left = (dg_t, du_t, hid_t)[which]
        out = (wg, wu, wd)[which]
        for k in range(NK):
            lo, v = k * CW, VALID[k]
            out[b * GB : (b + 1) * GB, lo : lo + v] = dot(
                left[b * GB : (b + 1) * GB, :], flat(xd, k, which // 2)[:, 0:v]
            ).astype(BF)

    fill = [lambda w=w, b=b: grad(w, b) for w in (2, 0, 1) for b in range(NG)]

    def filler():
        if fill:
            fill.pop(0)()

    for step in range(NK + 5):
        if step < NK:
            partial(step)
        if step == 0:
            hid_t[...] = gate_a[...].T.astype(BF)
            dg_t[...] = dg[...].T
            du_t[...] = du[...].T
        if 0 <= step - 1 < NK:
            back_core(step - 1)
        if 0 <= step - 2 < NK:
            back_pair(step - 2)
        if step >= 2 and (len(fill) > 2 * NG or step >= NK - 1):
            filler()
        if 0 <= step - 3 < NK:
            back_token(step - 3)
        if 0 <= step - 4 < NK:
            back_x(step - 4)
        if 0 <= step - 5 < NK:
            back_last(step - 5)
    while fill:
        filler()

    total = jnp.zeros((TOK, 1), F32)
    for k in range(NK):
        for r in range(2):
            lo = k * CW + r * HW
            v = max(0, min(HW, D - lo))
            if v:
                u = dn[2 * k + r, :, 0:v] * gain(lo, v)
                dn[2 * k + r, :, 0:v] = u
                total = total + jnp.sum(tf[:, lo : lo + v] * u, axis=-1, keepdims=True)
    mixed = rstd * rstd * rstd * (total / D)
    for k in range(NK):
        for r in range(2):
            lo = k * CW + r * HW
            v = max(0, min(HW, D - lo))
            if v:
                dtok_ref[:, lo : lo + v] = (
                    rstd * dn[2 * k + r, :, 0:v] - tf[:, lo : lo + v] * mixed
                ).astype(BF)

    for cp in sends:
        cp.wait_send()


def n_sends():
    early = sum(EARLY)
    late = NK - early
    n = early + (1 if early else 0)
    n += 7 * (late + 2 * early) + 7 * (2 if early else 1)
    n += 7 * (late + 2 * early) + 2 * late + 4 * NK
    n += NK + 2 * late + 7 * (late + 2 * early) + 7 * (late + 2 * early) + early
    return n


def write_out(a, b, c, a_hbm, b_hbm, c_hbm, sem):
    copies = [
        pltpu.make_async_copy(src, dst, sem.at[i])
        for i, (src, dst) in enumerate(((a, a_hbm), (b, b_hbm), (c, c_hbm)))
    ]
    for cp in copies:
        cp.start()
    for cp in copies:
        cp.wait()


def local(tokens, norm_gain, expert_ids, combine_weight, cotangent, w_gate, w_up, w_down):
    vm = pl.BlockSpec(memory_space=pltpu.VMEM)
    hbm = pl.BlockSpec(memory_space=pl.ANY)
    dma = pltpu.SemaphoreType.DMA
    scratch = [
        pltpu.VMEM((NK, 2, 2, TOK, CW), BF),
        pltpu.VMEM((2, 8, 256), F32), pltpu.VMEM((2, 8, 8, 256), F32),
        pltpu.VMEM((NK, 2, 256, CW), BF),
        pltpu.VMEM((NK, 2, ROWS, 8, CW), BF),
        pltpu.VMEM((NK, 2, TOTAL // 8, 8, CW), BF),
        pltpu.VMEM((8 * ROWS, 256), F32), pltpu.VMEM((2, 8 * ROWS, 256), BF),
        pltpu.VMEM((2, 8 * ROWS, 128), F32),
        pltpu.VMEM((TOTAL, FQ), F32), pltpu.VMEM((TOTAL, FQ), F32), pltpu.VMEM((TOTAL, FQ), F32),
        pltpu.VMEM((TOTAL, FQ), BF), pltpu.VMEM((TOTAL, FQ), BF),
        pltpu.VMEM((FQ, TOTAL), BF), pltpu.VMEM((FQ, TOTAL), BF), pltpu.VMEM((FQ, TOTAL), BF),
        pltpu.VMEM((NK, 2, TOTAL, HW), BF),
        pltpu.VMEM((NK, TOTAL, HW), BF),
        pltpu.VMEM((NK, TOTAL // 8, 8, HW), BF),
        pltpu.VMEM((NK, BLK // 4, 8, HW), BF), pltpu.VMEM((NK, BLK // 4, 8, HW), BF),
        pltpu.VMEM((NK, 2, ROWS, 8, HW), BF), pltpu.VMEM((NK, 2, 256, HW), BF),
        pltpu.VMEM((NK, 2, 8, TOK, HW), BF),
        pltpu.VMEM((NK, 2, TOK, HW), BF), pltpu.VMEM((NK, 2, TOK, HW), BF),
        pltpu.VMEM((2 * NK, TOK, HW), F32),
        dma((3,)), dma((1,)), dma((2, 8)), dma((1,)), dma((NK + 1,)), dma((1,)), dma((NK, 2, 8)),
        dma((NK, 2, 2, 4)), dma((NK, 2)), dma((NK, 4)), dma((NK,)), dma((NK, 2)), dma((NK, 2, 8)),
        dma((NK, 2, 8)), dma((NK,)), dma((n_sends(),)),
    ]
    d_tokens, grad_gate, grad_up, grad_down = pl.pallas_call(
        kernel,
        out_shape=(
            jax.ShapeDtypeStruct((TOK, D), BF),
            pltpu.VMEM((1, FQ, D), BF),
            pltpu.VMEM((1, FQ, D), BF),
            pltpu.VMEM((1, FQ, D), BF),
        ),
        in_specs=[vm, vm, vm, vm, vm, hbm, hbm, hbm],
        out_specs=(vm, vm, vm, vm),
        scratch_shapes=scratch,
        compiler_params=pltpu.CompilerParams(
            collective_id=0, has_side_effects=True, vmem_limit_bytes=48 << 20
        ),
    )(
        tokens, norm_gain, expert_ids.T, combine_weight.T, cotangent,
        jnp.swapaxes(w_gate, 1, 2), jnp.swapaxes(w_up, 1, 2), w_down,
    )
    grad_gate, grad_up, grad_down = pl.pallas_call(
        write_out,
        out_shape=(jax.ShapeDtypeStruct((1, FQ, D), BF),) * 3,
        in_specs=[vm] * 3,
        out_specs=(hbm,) * 3,
        scratch_shapes=[dma((3,))],
        compiler_params=pltpu.CompilerParams(has_side_effects=True, vmem_limit_bytes=1 << 20),
    )(grad_gate, grad_up, grad_down)
    return d_tokens, jnp.swapaxes(grad_gate, 1, 2), jnp.swapaxes(grad_up, 1, 2), grad_down


def solution(mesh):
    placed = (
        P("sq", None),
        P(),
        P("sq", None),
        P("sq", None),
        P("sq", None),
        P("sq", None, None),
        P("sq", None, None),
        P("sq", None, None),
    )
    return jax.shard_map(
        local,
        mesh=mesh,
        in_specs=placed,
        out_specs=(P("sq", None), P("sq", None, None), P("sq", None, None), P("sq", None, None)),
        check_vma=False,
    )
```

```python
import functools

import jax
import jax.numpy as jnp
from jax import lax
from jax.experimental import pallas as pl
from jax.experimental.pallas import tpu as pltpu
from jax.sharding import PartitionSpec as P

MESH = pl.DeviceIdType.MESH
BF = jnp.bfloat16
F32 = jnp.float32

eps = 1e-05
alpha = 1.702

D = 2880
FQ = 720
TOK = 32
TOP = 4
SLOTS = 5
CW = 512
HW = CW // 2
NK = -(-D // CW)
VALID = [min(CW, D - k * CW) for k in range(NK)]
LANES = [-(-v // 128) * 128 for v in VALID]
EARLY = [False, False, False, True, True, False]
WINDOW = 3
AHEAD = (1, 3, 4)
BACK = (1, 3, 5, 7, 8)
ROWS = 8 * SLOTS
BLK = 4 * ROWS
TOTAL = 4 * BLK
NG = 3
GB = FQ // NG


def dot(a, b):
    return jnp.dot(a, b, preferred_element_type=F32)


def dot_t(a, b):
    return lax.dot_general(a, b, (((1,), (1,)), ((), ())), preferred_element_type=F32)


def dot_0(a, b):
    return lax.dot_general(a, b, (((0,), (0,)), ((), ())), preferred_element_type=F32)


def device(x, z, y, c):
    return (((x * 4 + z) * 4 + y) * 2 + c,)


def kernel(
    tok_hbm, gain_hbm, ids_hbm, cw_hbm, cot_hbm, wg_hbm, wu_hbm, wd_hbm,
    dtok_ref, gg_ref, gu_ref, gd_ref,
    tok_ref, gain_ref, ids_ref, cw_ref, cot_ref, own, meta_own, meta_got, gath, rows, xd, sel_f, sel, scale, up_a, gate_a, dhid_a,
    dg, du, dg_t, du_t, hid_t, part, part_got, psum, h_got, drow, z_got, tsum, x_got, f_out, f_got, dn,
    wsem, isem, msem, msend, fsem, hsem, xsem, zsem, ysem, csem, rcsem, rhsem, rzsem, rxsem, rfsem,
    send,
):
    me = lax.axis_index("sq")
    c = lax.rem(me, 2)
    y = lax.rem(me // 2, 4)
    z = lax.rem(me // 8, 4)
    x = me // 32
    h = lax.rem(y, 2)
    half = y // 2
    yp = y + 1 - 2 * h
    yl = 3 - y
    any_early = any(EARLY)

    wg, wu, wd = gg_ref.at[0], gu_ref.at[0], gd_ref.at[0]
    weights = [
        pltpu.make_async_copy(wg_hbm.at[0], wg, wsem.at[0]),
        pltpu.make_async_copy(wu_hbm.at[0], wu, wsem.at[1]),
        pltpu.make_async_copy(wd_hbm.at[0], wd, wsem.at[2]),
    ]
    inputs = [
        pltpu.make_async_copy(src, dst, isem.at[i])
        for i, (src, dst) in enumerate(
            (
                (tok_hbm, tok_ref), (gain_hbm, gain_ref), (ids_hbm, ids_ref),
                (cw_hbm, cw_ref), (cot_hbm, cot_ref),
            )
        )
    ]
    for cp in inputs:
        cp.start()

    peers_x = [(dx, dr) for dx in range(4) for dr in range(2) if (dx, dr) != (0, 0)]
    peers_z = [(dz, pr) for dz in range(4) for pr in range(2) if (dz, pr) != (0, 0)]

    def x_peer(dx, dr):
        return lax.rem(x + dx, 4), lax.rem(c + dr, 2)

    def z_peer(dz, pr):
        return lax.rem(z + dz, 4), (yl if pr else y)

    barrier = pltpu.get_barrier_semaphore()
    for p in peers_x:
        xx, cc = x_peer(*p)
        pl.semaphore_signal(barrier, inc=1, device_id=device(xx, z, y, cc), device_id_type=MESH)
    for p in peers_z:
        zz, yy = z_peer(*p)
        pl.semaphore_signal(barrier, inc=1, device_id=device(x, zz, yy, c), device_id_type=MESH)
    pl.semaphore_signal(barrier, inc=1, device_id=device(x, z, yp, c), device_id_type=MESH)

    def gain(lo, v):
        return gain_ref[pl.ds(lo, v)].reshape(1, v)

    for cp in inputs:
        cp.wait()

    tf = tok_ref[...].astype(F32)
    rstd = lax.rsqrt(jnp.mean(tf * tf, axis=-1, keepdims=True) + eps)
    for k in range(NK):
        lo, v, n = k * CW, VALID[k], LANES[k]
        if v < n:
            own[k, 0, h, :, :] = jnp.zeros((TOK, CW), BF)
            own[k, 1, h, :, :] = jnp.zeros((TOK, CW), BF)
        own[k, 0, h, :, 0:v] = (tf[:, lo : lo + v] * rstd * gain(lo, v)).astype(BF)
        own[k, 1, h, :, 0:v] = cot_ref[:, lo : lo + v]

    lane = lax.broadcasted_iota(jnp.int32, (TOK, 256), 1)
    trow = lax.broadcasted_iota(jnp.int32, (TOK, 256), 0)
    place = jnp.where(lane == trow + TOK * (2 * x + c), 1.0, 0.0).astype(BF)
    w_all = cw_ref[...]
    w_hi = w_all.astype(BF)
    w_rest = w_all - w_hi.astype(F32)
    w_mid = w_rest.astype(BF)
    w_lo = (w_rest - w_mid.astype(F32)).astype(BF)
    meta_own[h, 0:TOP, :] = dot(ids_ref[...].astype(F32).astype(BF), place)
    meta_own[h, TOP : 2 * TOP, :] = dot(w_hi, place) + dot(w_mid, place) + dot(w_lo, place)

    pl.semaphore_wait(barrier, len(peers_x) + len(peers_z) + 1)

    sends = []
    count = [0]

    def put(src, dst, recv, dev):
        cp = pltpu.make_async_remote_copy(
            src_ref=src, dst_ref=dst, send_sem=send.at[count[0]], recv_sem=recv,
            device_id=dev, device_id_type=MESH,
        )
        count[0] += 1
        cp.start()
        sends.append(cp)

    def arrived(dst, sem):
        pltpu.make_async_copy(dst, dst, sem).wait()

    src_mine = 2 * x + c

    for k in range(NK):
        if EARLY[k]:
            n = LANES[k]
            o = own.at[k, :, h, :, pl.ds(0, n)]
            put(o, o, fsem.at[k], device(x, z, yp, c))
    if any_early:
        put(meta_own.at[h], meta_own.at[h], fsem.at[NK], device(x, z, yp, c))

    def slabs(ref, index, row, count, n):
        return ref.at[(*index, pl.ds(row // 8, count // 8), slice(None), pl.ds(0, n))]

    def flat(ref, *index):
        r = ref.at[index]
        return r.reshape(r.shape[0] * 8, r.shape[2])

    def send_x(k):
        n = LANES[k]
        hs = [0, 1] if EARLY[k] else [h]
        if EARLY[k]:
            o = own.at[k, :, 1 - h, :, pl.ds(0, n)]
            arrived(o, fsem.at[k])
        for i, hh in enumerate(hs):
            for p in peers_x:
                xx, cc = x_peer(*p)
                put(
                    own.at[k, cc, hh, :, pl.ds(0, n)],
                    gath.at[k, hh, pl.ds(TOK * src_mine, TOK), pl.ds(0, n)],
                    xsem.at[k, i, src_mine],
                    device(xx, z, y, cc),
                )
            pltpu.make_async_copy(
                own.at[k, c, hh, :, pl.ds(0, n)],
                gath.at[k, hh, pl.ds(TOK * src_mine, TOK), pl.ds(0, n)],
                xsem.at[k, i, src_mine],
            ).start()

    hs_meta = [0, 1] if any_early else [h]

    def send_meta():
        if any_early:
            arrived(meta_own.at[1 - h], fsem.at[NK])
        for i, hh in enumerate(hs_meta):
            for p in peers_x:
                xx, cc = x_peer(*p)
                put(
                    meta_own.at[hh], meta_got.at[hh, src_mine], msem.at[i, src_mine],
                    device(xx, z, y, cc),
                )
            pltpu.make_async_copy(
                meta_own.at[hh], meta_got.at[hh, src_mine], msem.at[i, src_mine]
            ).start()

    if EARLY[0] or not any_early:
        send_meta()
        send_x(0)
    else:
        send_x(0)
        send_meta()
    for k in range(1, WINDOW):
        send_x(k)

    for w in weights:
        w.start()

    def build():
        e_of = lax.broadcasted_iota(jnp.int32, (8, 256), 0).astype(F32) + (8 * x).astype(F32)
        t1 = lax.broadcasted_iota(jnp.int32, (256, 256), 0)
        t2 = lax.broadcasted_iota(jnp.int32, (256, 256), 1)
        lower = jnp.where((t1 < t2) & (t1 // TOK == t2 // TOK), 1.0, 0.0).astype(BF)
        r = lax.broadcasted_iota(jnp.int32, (ROWS, 256), 0)
        t = lax.broadcasted_iota(jnp.int32, (ROWS, 256), 1)
        src_ok = r // SLOTS == t // TOK
        slot_of = lax.rem(r, SLOTS).astype(F32)
        for i, hh in enumerate(hs_meta):
            for s in range(8):
                arrived(meta_got.at[hh, s], msem.at[i, s])
            meta = meta_got[hh, 0]
            for s in range(1, 8):
                meta = meta + meta_got[hh, s]
            named = jnp.zeros((8, 256), F32)
            weight = jnp.zeros((8, 256), F32)
            for j in range(TOP):
                hit = meta[j : j + 1, :] == e_of
                named = named + jnp.where(hit, 1.0, 0.0)
                weight = weight + jnp.where(hit, meta[TOP + j : TOP + j + 1, :], 0.0)
            rank = dot(named.astype(BF), lower)
            for e in range(8):
                on = src_ok & (rank[e : e + 1, :] == slot_of)
                one = jnp.where(on, jnp.broadcast_to(named[e : e + 1, :], (ROWS, 256)), 0.0)
                sel_f[pl.ds(e * ROWS, ROWS), :] = one
                w_row = jnp.sum(one * weight[e : e + 1, :], axis=-1, keepdims=True)
                scale[hh, pl.ds(e * ROWS, ROWS), :] = jnp.broadcast_to(
                    jnp.where(c == 0, jnp.ones_like(w_row), w_row), (ROWS, 128)
                )
            sel[hh, :, :] = sel_f[...].astype(BF)

    def select(k):
        n = LANES[k]
        hs = [0, 1] if EARLY[k] else [h]
        for i, hh in enumerate(hs):
            for s in range(8):
                arrived(gath.at[k, hh, pl.ds(TOK * s, TOK), pl.ds(0, n)], xsem.at[k, i, s])
        if k + WINDOW < NK:
            send_x(k + WINDOW)
        for i, hh in enumerate(hs):
            picked = dot(sel[hh], gath[k, hh, :, 0:n])
            picked = (picked * scale[hh, :, 0:1]).astype(BF)
            flat(rows, k, hh)[:, 0:n] = picked
            ys = 2 * half + hh if EARLY[k] else y
            for dz in range(4):
                for pr in range(2):
                    zz, yy = z_peer(dz, pr)
                    pp = half + pr * (1 - 2 * half)
                    src = slabs(rows, (k, hh), (zz * 2 + pp) * ROWS, ROWS, n)
                    dst = slabs(xd, (k, c), ys * BLK + z * ROWS, ROWS, n)
                    sem = zsem.at[k, i, pr, z]
                    if dz == 0 and pr == 0:
                        pltpu.make_async_copy(src, dst, sem).start()
                    else:
                        put(src, dst, sem, device(x, zz, yy, c))

    def block(k, ys):
        return slabs(xd, (k, c), ys * BLK, BLK, LANES[k])

    def wait_z(k, i, pr, ys):
        n = LANES[k]
        for s in range(4):
            arrived(slabs(xd, (k, c), ys * BLK + s * ROWS, ROWS, n), zsem.at[k, i, pr, s])

    def to_core(k, ys):
        put(block(k, ys), block(k, ys), csem.at[k, ys], device(x, z, y, 1 - c))

    def forward(k):
        if EARLY[k]:
            for pr in range(2):
                for i in range(2):
                    ys = 2 * (half + pr * (1 - 2 * half)) + i
                    wait_z(k, i, pr, ys)
                    to_core(k, ys)
        else:
            for pr, ys in enumerate((y, yl)):
                wait_z(k, 0, pr, ys)
                put(block(k, ys), block(k, ys), ysem.at[k, pr], device(x, z, yp, c))
                to_core(k, ys)

    def finish(k):
        if not EARLY[k]:
            for pr, ys in enumerate((yp, 3 - yp)):
                arrived(block(k, ys), ysem.at[k, pr])
                to_core(k, ys)

    def up_matmuls(k):
        n, v, lo = LANES[k], VALID[k], k * CW
        for ys in range(4):
            arrived(slabs(xd, (k, 1 - c), ys * BLK, BLK, n), csem.at[k, ys])
        if k == 0:
            for w in weights:
                w.wait()
        xs = flat(xd, k, 0)[:, 0:v]
        gate = dot_t(xs, wg[:, lo : lo + v])
        gate_a[...] = gate if k == 0 else gate_a[...] + gate
        up = dot_t(xs, wu[:, lo : lo + v])
        up_a[...] = up if k == 0 else up_a[...] + up
        dhid = dot_t(flat(xd, k, 1)[:, 0:v], wd[:, lo : lo + v])
        dhid_a[...] = dhid if k == 0 else dhid_a[...] + dhid

    build()
    for step in range(NK + AHEAD[2]):
        if step < NK:
            select(step)
        for stage, after in zip((forward, finish, up_matmuls), AHEAD, strict=True):
            if 0 <= step - after < NK:
                stage(step - after)

    def pointwise(i, carry):
        b = pl.ds(pl.multiple_of(i * BLK, BLK), BLK)
        gate = gate_a[b, :]
        sig = jax.nn.sigmoid(alpha * gate)
        glu = gate * sig
        up1 = up_a[b, :] + 1.0
        gate_a[b, :] = glu * up1
        d_hid = dhid_a[b, :]
        du[b, :] = (d_hid * glu).astype(BF)
        dg[b, :] = (d_hid * up1 * (sig + alpha * gate * sig * (1.0 - sig))).astype(BF)
        return carry

    lax.fori_loop(0, 4, pointwise, 0)

    def partial(k):
        lo, v = k * CW, VALID[k]
        if v < CW:
            part[k, 1, :, :] = jnp.zeros((TOTAL, HW), BF)
        p = dot(dg[...], wg[:, lo : lo + v]) + dot(du[...], wu[:, lo : lo + v])
        p = p.astype(BF)
        part[k, 0, :, :] = p[:, 0:HW]
        part[k, 1, :, 0 : v - HW] = p[:, HW:v]
        put(part.at[k, 1 - c], part_got.at[k], rcsem.at[k], device(x, z, y, 1 - c))

    def back_z(k, src_ref, base_of):
        for pr in range(2):
            ydst = yl if pr else y
            his = [0, 1] if EARLY[k] else [0]
            for i in his:
                hd = i if EARLY[k] else lax.rem(ydst, 2)
                for dz in range(4):
                    zz = lax.rem(z + dz, 4)
                    src = slabs(src_ref, (k,), base_of(pr, i) * BLK + zz * ROWS, ROWS, HW)
                    dst = slabs(z_got, (k, hd), (z * 2 + half) * ROWS, ROWS, HW)
                    sem = rzsem.at[k, i, z * 2 + half]
                    if dz == 0 and pr == 0:
                        pltpu.make_async_copy(src, dst, sem).start()
                    else:
                        put(src, dst, sem, device(x, zz, ydst, c))

    def back_core(k):
        arrived(part_got.at[k], rcsem.at[k])
        flat(psum, k)[...] = (part[k, c].astype(F32) + part_got[k].astype(F32)).astype(BF)
        if EARLY[k]:
            back_z(k, psum, lambda pr, i: 2 * (half + pr * (1 - 2 * half)) + i)
        else:
            for j, ys in enumerate((yp, 3 - yp)):
                put(
                    slabs(psum, (k,), ys * BLK, BLK, HW), slabs(h_got, (k,), j * BLK, BLK, HW),
                    rhsem.at[k, j], device(x, z, yp, c),
                )

    def back_pair(k):
        if not EARLY[k]:
            for j, ys in enumerate((y, yl)):
                arrived(slabs(h_got, (k,), j * BLK, BLK, HW), rhsem.at[k, j])
                b = pl.ds(pl.multiple_of(ys * BLK, BLK), BLK)
                to = pl.ds(j * BLK, BLK)
                flat(drow, k)[to, :] = (
                    flat(psum, k)[b, :].astype(F32) + flat(h_got, k)[to, :].astype(F32)
                ).astype(BF)
            back_z(k, drow, lambda pr, i: pr)

    def back_token(k):
        hs = [0, 1] if EARLY[k] else [h]
        for i, hh in enumerate(hs):
            for e in range(8):
                arrived(slabs(z_got, (k, hh), e * ROWS, ROWS, HW), rzsem.at[k, i, e])
        for i, hh in enumerate(hs):
            tsum[k, hh, :, :] = dot_0(sel[hh], flat(z_got, k, hh)[...]).astype(BF)
            for p in peers_x:
                xx, cc = x_peer(*p)
                put(
                    tsum.at[k, hh, pl.ds((2 * xx + cc) * TOK, TOK), :],
                    x_got.at[k, hh, src_mine],
                    rxsem.at[k, i, src_mine],
                    device(xx, z, y, cc),
                )
            pltpu.make_async_copy(
                tsum.at[k, hh, pl.ds(src_mine * TOK, TOK), :],
                x_got.at[k, hh, src_mine],
                rxsem.at[k, i, src_mine],
            ).start()

    def gather_sum(k, hh, r):
        s = x_got[k, hh, r].astype(F32)
        for j in range(1, 4):
            s = s + x_got[k, hh, 2 * j + r].astype(F32)
        return s

    def back_x(k):
        hs = [0, 1] if EARLY[k] else [h]
        for i, hh in enumerate(hs):
            for s in range(8):
                arrived(x_got.at[k, hh, s], rxsem.at[k, i, s])
        for r in range(2):
            dn[2 * k + r] = gather_sum(k, h, r)
        if EARLY[k]:
            for r in range(2):
                f_out[k, r] = gather_sum(k, 1 - h, r).astype(BF)
            put(f_out.at[k], f_got.at[k], rfsem.at[k], device(x, z, yp, c))

    def back_last(k):
        if EARLY[k]:
            arrived(f_got.at[k], rfsem.at[k])
            for r in range(2):
                dn[2 * k + r] = dn[2 * k + r] + f_got[k, r].astype(F32)

    def grad(which, b):
        left = (dg_t, du_t, hid_t)[which]
        out = (wg, wu, wd)[which]
        for k in range(NK):
            lo, v = k * CW, VALID[k]
            out[b * GB : (b + 1) * GB, lo : lo + v] = dot(
                left[b * GB : (b + 1) * GB, :], flat(xd, k, which // 2)[:, 0:v]
            ).astype(BF)

    fill = [lambda w=w, b=b: grad(w, b) for w in (2, 0, 1) for b in range(NG)]

    for step in range(NK + BACK[-1]):
        if step < NK:
            partial(step)
        if step == 0:
            hid_t[...] = gate_a[...].T.astype(BF)
            dg_t[...] = dg[...].T
            du_t[...] = du[...].T
        for i, stage in enumerate((back_core, back_pair, back_token, back_x, back_last)):
            if 0 <= step - BACK[i] < NK:
                stage(step - BACK[i])
            if i == 1 and step >= 2 and (len(fill) > 2 * NG or step >= NK - 1) and fill:
                fill.pop(0)()
    while fill:
        fill.pop(0)()

    total = jnp.zeros((TOK, 1), F32)
    for k in range(NK):
        for r in range(2):
            lo = k * CW + r * HW
            v = max(0, min(HW, D - lo))
            if v:
                u = dn[2 * k + r, :, 0:v] * gain(lo, v)
                dn[2 * k + r, :, 0:v] = u
                total = total + jnp.sum(tf[:, lo : lo + v] * u, axis=-1, keepdims=True)
    mixed = rstd * rstd * rstd * (total / D)
    for k in range(NK):
        for r in range(2):
            lo = k * CW + r * HW
            v = max(0, min(HW, D - lo))
            if v:
                dtok_ref[:, lo : lo + v] = (
                    rstd * dn[2 * k + r, :, 0:v] - tf[:, lo : lo + v] * mixed
                ).astype(BF)

    for cp in sends:
        cp.wait_send()


def n_sends():
    early = sum(EARLY)
    late = NK - early
    n = early + (1 if early else 0)
    n += 7 * (late + 2 * early) + 7 * (2 if early else 1)
    n += 7 * (late + 2 * early) + 2 * late + 4 * NK
    n += NK + 2 * late + 7 * (late + 2 * early) + 7 * (late + 2 * early) + early
    return n


def write_out(t, a, b, c, t_hbm, a_hbm, b_hbm, c_hbm, sem):
    copies = [
        pltpu.make_async_copy(src, dst, sem.at[i])
        for i, (src, dst) in enumerate(((t, t_hbm), (a, a_hbm), (b, b_hbm), (c, c_hbm)))
    ]
    for cp in copies:
        cp.start()
    for cp in copies:
        cp.wait()


def local(tokens, norm_gain, expert_ids, combine_weight, cotangent, w_gate, w_up, w_down):
    vm = pl.BlockSpec(memory_space=pltpu.VMEM)
    hbm = pl.BlockSpec(memory_space=pl.ANY)
    dma = pltpu.SemaphoreType.DMA
    scratch = [
        pltpu.VMEM((TOK, D), BF), pltpu.VMEM((D,), F32), pltpu.VMEM((TOP, TOK), jnp.int32),
        pltpu.VMEM((TOP, TOK), F32), pltpu.VMEM((TOK, D), BF),
        pltpu.VMEM((NK, 2, 2, TOK, CW), BF),
        pltpu.VMEM((2, 8, 256), F32), pltpu.VMEM((2, 8, 8, 256), F32),
        pltpu.VMEM((NK, 2, 256, CW), BF),
        pltpu.VMEM((NK, 2, ROWS, 8, CW), BF),
        pltpu.VMEM((NK, 2, TOTAL // 8, 8, CW), BF),
        pltpu.VMEM((8 * ROWS, 256), F32), pltpu.VMEM((2, 8 * ROWS, 256), BF),
        pltpu.VMEM((2, 8 * ROWS, 128), F32),
        pltpu.VMEM((TOTAL, FQ), F32), pltpu.VMEM((TOTAL, FQ), F32), pltpu.VMEM((TOTAL, FQ), F32),
        pltpu.VMEM((TOTAL, FQ), BF), pltpu.VMEM((TOTAL, FQ), BF),
        pltpu.VMEM((FQ, TOTAL), BF), pltpu.VMEM((FQ, TOTAL), BF), pltpu.VMEM((FQ, TOTAL), BF),
        pltpu.VMEM((NK, 2, TOTAL, HW), BF),
        pltpu.VMEM((NK, TOTAL, HW), BF),
        pltpu.VMEM((NK, TOTAL // 8, 8, HW), BF),
        pltpu.VMEM((NK, BLK // 4, 8, HW), BF), pltpu.VMEM((NK, BLK // 4, 8, HW), BF),
        pltpu.VMEM((NK, 2, ROWS, 8, HW), BF), pltpu.VMEM((NK, 2, 256, HW), BF),
        pltpu.VMEM((NK, 2, 8, TOK, HW), BF),
        pltpu.VMEM((NK, 2, TOK, HW), BF), pltpu.VMEM((NK, 2, TOK, HW), BF),
        pltpu.VMEM((2 * NK, TOK, HW), F32),
        dma((3,)), dma((5,)), dma((2, 8)), dma((1,)), dma((NK + 1,)), dma((1,)), dma((NK, 2, 8)),
        dma((NK, 2, 2, 4)), dma((NK, 2)), dma((NK, 4)), dma((NK,)), dma((NK, 2)), dma((NK, 2, 8)),
        dma((NK, 2, 8)), dma((NK,)), dma((n_sends(),)),
    ]
    d_tokens, grad_gate, grad_up, grad_down = pl.pallas_call(
        kernel,
        out_shape=(
            pltpu.VMEM((TOK, D), BF),
            pltpu.VMEM((1, FQ, D), BF),
            pltpu.VMEM((1, FQ, D), BF),
            pltpu.VMEM((1, FQ, D), BF),
        ),
        in_specs=[hbm] * 8,
        out_specs=(vm, vm, vm, vm),
        scratch_shapes=scratch,
        compiler_params=pltpu.CompilerParams(
            collective_id=0, has_side_effects=True, vmem_limit_bytes=48 << 20
        ),
    )(
        tokens, norm_gain, expert_ids.T, combine_weight.T, cotangent,
        jnp.swapaxes(w_gate, 1, 2), jnp.swapaxes(w_up, 1, 2), w_down,
    )
    d_tokens, grad_gate, grad_up, grad_down = pl.pallas_call(
        write_out,
        out_shape=(jax.ShapeDtypeStruct((TOK, D), BF),)
        + (jax.ShapeDtypeStruct((1, FQ, D), BF),) * 3,
        in_specs=[vm] * 4,
        out_specs=(hbm,) * 4,
        scratch_shapes=[dma((4,))],
        compiler_params=pltpu.CompilerParams(has_side_effects=True, vmem_limit_bytes=1 << 20),
    )(d_tokens, grad_gate, grad_up, grad_down)
    return d_tokens, jnp.swapaxes(grad_gate, 1, 2), jnp.swapaxes(grad_up, 1, 2), grad_down


def solution(mesh):
    placed = (
        P("sq", None),
        P(),
        P("sq", None),
        P("sq", None),
        P("sq", None),
        P("sq", None, None),
        P("sq", None, None),
        P("sq", None, None),
    )
    return jax.shard_map(
        local,
        mesh=mesh,
        in_specs=placed,
        out_specs=(P("sq", None), P("sq", None, None), P("sq", None, None), P("sq", None, None)),
        check_vma=False,
    )
```

```python
import functools

import jax
import jax.numpy as jnp
from jax import lax
from jax.experimental import pallas as pl
from jax.experimental.pallas import tpu as pltpu
from jax.sharding import PartitionSpec as P

MESH = pl.DeviceIdType.MESH
BF = jnp.bfloat16
F32 = jnp.float32

eps = 1e-05
alpha = 1.702

D = 2880
FQ = 720
TOK = 32
TOP = 4
SLOTS = 5
CW = 512
HW = CW // 2
NK = -(-D // CW)
VALID = [min(CW, D - k * CW) for k in range(NK)]
LANES = [-(-v // 128) * 128 for v in VALID]
EARLY = [False, False, False, True, True, False]
WINDOW = 3
AHEAD = (1, 3, 4)
BACK = (1, 4, 6, 8, 9)
ROWS = 8 * SLOTS
BLK = 4 * ROWS
TOTAL = 4 * BLK
NG = 3
GB = FQ // NG


def dot(a, b):
    return jnp.dot(a, b, preferred_element_type=F32)


def dot_t(a, b):
    return lax.dot_general(a, b, (((1,), (1,)), ((), ())), preferred_element_type=F32)


def dot_0(a, b):
    return lax.dot_general(a, b, (((0,), (0,)), ((), ())), preferred_element_type=F32)


def device(x, z, y, c):
    return (((x * 4 + z) * 4 + y) * 2 + c,)


def kernel(
    tok_hbm, gain_hbm, ids_hbm, cw_hbm, cot_hbm, wg_hbm, wu_hbm, wd_hbm,
    dtok_ref, gg_ref, gu_ref, gd_ref,
    tok_ref, gain_ref, ids_ref, cw_ref, cot_ref, own, meta_own, meta_got, gath, rows, xd, sel_f, sel, scale, up_a, gate_a, dhid_a,
    dg, du, dg_t, du_t, hid_t, part, part_got, psum, h_got, drow, z_got, tsum, x_got, f_out, f_got, dn,
    wsem, isem, msem, msend, fsem, hsem, xsem, zsem, ysem, csem, rcsem, rhsem, rzsem, rxsem, rfsem,
    send,
):
    me = lax.axis_index("sq")
    c = lax.rem(me, 2)
    y = lax.rem(me // 2, 4)
    z = lax.rem(me // 8, 4)
    x = me // 32
    h = lax.rem(y, 2)
    half = y // 2
    yp = y + 1 - 2 * h
    yl = 3 - y
    any_early = any(EARLY)

    wg, wu, wd = gg_ref.at[0], gu_ref.at[0], gd_ref.at[0]
    weights = [
        pltpu.make_async_copy(wg_hbm.at[0], wg, wsem.at[0]),
        pltpu.make_async_copy(wu_hbm.at[0], wu, wsem.at[1]),
        pltpu.make_async_copy(wd_hbm.at[0], wd, wsem.at[2]),
    ]
    inputs = [
        pltpu.make_async_copy(src, dst, isem.at[i])
        for i, (src, dst) in enumerate(
            (
                (tok_hbm, tok_ref), (gain_hbm, gain_ref), (ids_hbm, ids_ref),
                (cw_hbm, cw_ref), (cot_hbm, cot_ref),
            )
        )
    ]
    for cp in inputs:
        cp.start()

    peers_x = [(dx, dr) for dx in range(4) for dr in range(2) if (dx, dr) != (0, 0)]
    peers_z = [(dz, pr) for dz in range(4) for pr in range(2) if (dz, pr) != (0, 0)]

    def x_peer(dx, dr):
        return lax.rem(x + dx, 4), lax.rem(c + dr, 2)

    def z_peer(dz, pr):
        return lax.rem(z + dz, 4), (yl if pr else y)

    barrier = pltpu.get_barrier_semaphore()
    for p in peers_x:
        xx, cc = x_peer(*p)
        pl.semaphore_signal(barrier, inc=1, device_id=device(xx, z, y, cc), device_id_type=MESH)
    for p in peers_z:
        zz, yy = z_peer(*p)
        pl.semaphore_signal(barrier, inc=1, device_id=device(x, zz, yy, c), device_id_type=MESH)
    pl.semaphore_signal(barrier, inc=1, device_id=device(x, z, yp, c), device_id_type=MESH)

    def gain(lo, v):
        return gain_ref[pl.ds(lo, v)].reshape(1, v)

    for cp in inputs:
        cp.wait()

    tf = tok_ref[...].astype(F32)
    rstd = lax.rsqrt(jnp.mean(tf * tf, axis=-1, keepdims=True) + eps)
    for k in range(NK):
        lo, v, n = k * CW, VALID[k], LANES[k]
        if v < n:
            own[k, 0, h, :, :] = jnp.zeros((TOK, CW), BF)
            own[k, 1, h, :, :] = jnp.zeros((TOK, CW), BF)
        own[k, 0, h, :, 0:v] = (tf[:, lo : lo + v] * rstd * gain(lo, v)).astype(BF)
        own[k, 1, h, :, 0:v] = cot_ref[:, lo : lo + v]

    lane = lax.broadcasted_iota(jnp.int32, (TOK, 256), 1)
    trow = lax.broadcasted_iota(jnp.int32, (TOK, 256), 0)
    place = jnp.where(lane == trow + TOK * (2 * x + c), 1.0, 0.0).astype(BF)
    w_all = cw_ref[...]
    w_hi = w_all.astype(BF)
    w_rest = w_all - w_hi.astype(F32)
    w_mid = w_rest.astype(BF)
    w_lo = (w_rest - w_mid.astype(F32)).astype(BF)
    meta_own[h, 0:TOP, :] = dot(ids_ref[...].astype(F32).astype(BF), place)
    meta_own[h, TOP : 2 * TOP, :] = dot(w_hi, place) + dot(w_mid, place) + dot(w_lo, place)

    pl.semaphore_wait(barrier, len(peers_x) + len(peers_z) + 1)

    sends = []
    count = [0]

    def put(src, dst, recv, dev):
        cp = pltpu.make_async_remote_copy(
            src_ref=src, dst_ref=dst, send_sem=send.at[count[0]], recv_sem=recv,
            device_id=dev, device_id_type=MESH,
        )
        count[0] += 1
        cp.start()
        sends.append(cp)

    def arrived(dst, sem):
        pltpu.make_async_copy(dst, dst, sem).wait()

    src_mine = 2 * x + c

    for k in range(NK):
        if EARLY[k]:
            n = LANES[k]
            o = own.at[k, :, h, :, pl.ds(0, n)]
            put(o, o, fsem.at[k], device(x, z, yp, c))
    if any_early:
        put(meta_own.at[h], meta_own.at[h], fsem.at[NK], device(x, z, yp, c))

    def slabs(ref, index, row, count, n):
        return ref.at[(*index, pl.ds(row // 8, count // 8), slice(None), pl.ds(0, n))]

    def flat(ref, *index):
        r = ref.at[index]
        return r.reshape(r.shape[0] * 8, r.shape[2])

    def send_x(k):
        n = LANES[k]
        hs = [0, 1] if EARLY[k] else [h]
        if EARLY[k]:
            o = own.at[k, :, 1 - h, :, pl.ds(0, n)]
            arrived(o, fsem.at[k])
        for i, hh in enumerate(hs):
            for p in peers_x:
                xx, cc = x_peer(*p)
                put(
                    own.at[k, cc, hh, :, pl.ds(0, n)],
                    gath.at[k, hh, pl.ds(TOK * src_mine, TOK), pl.ds(0, n)],
                    xsem.at[k, i, src_mine],
                    device(xx, z, y, cc),
                )
            pltpu.make_async_copy(
                own.at[k, c, hh, :, pl.ds(0, n)],
                gath.at[k, hh, pl.ds(TOK * src_mine, TOK), pl.ds(0, n)],
                xsem.at[k, i, src_mine],
            ).start()

    hs_meta = [0, 1] if any_early else [h]

    def send_meta():
        if any_early:
            arrived(meta_own.at[1 - h], fsem.at[NK])
        for i, hh in enumerate(hs_meta):
            for p in peers_x:
                xx, cc = x_peer(*p)
                put(
                    meta_own.at[hh], meta_got.at[hh, src_mine], msem.at[i, src_mine],
                    device(xx, z, y, cc),
                )
            pltpu.make_async_copy(
                meta_own.at[hh], meta_got.at[hh, src_mine], msem.at[i, src_mine]
            ).start()

    if EARLY[0] or not any_early:
        send_meta()
        send_x(0)
    else:
        send_x(0)
        send_meta()
    for k in range(1, WINDOW):
        send_x(k)

    for w in weights:
        w.start()

    def build():
        e_of = lax.broadcasted_iota(jnp.int32, (8, 256), 0).astype(F32) + (8 * x).astype(F32)
        t1 = lax.broadcasted_iota(jnp.int32, (256, 256), 0)
        t2 = lax.broadcasted_iota(jnp.int32, (256, 256), 1)
        lower = jnp.where((t1 < t2) & (t1 // TOK == t2 // TOK), 1.0, 0.0).astype(BF)
        r = lax.broadcasted_iota(jnp.int32, (ROWS, 256), 0)
        t = lax.broadcasted_iota(jnp.int32, (ROWS, 256), 1)
        src_ok = r // SLOTS == t // TOK
        slot_of = lax.rem(r, SLOTS).astype(F32)
        for i, hh in enumerate(hs_meta):
            for s in range(8):
                arrived(meta_got.at[hh, s], msem.at[i, s])
            meta = meta_got[hh, 0]
            for s in range(1, 8):
                meta = meta + meta_got[hh, s]
            named = jnp.zeros((8, 256), F32)
            weight = jnp.zeros((8, 256), F32)
            for j in range(TOP):
                hit = meta[j : j + 1, :] == e_of
                named = named + jnp.where(hit, 1.0, 0.0)
                weight = weight + jnp.where(hit, meta[TOP + j : TOP + j + 1, :], 0.0)
            rank = dot(named.astype(BF), lower)
            for e in range(8):
                on = src_ok & (rank[e : e + 1, :] == slot_of)
                one = jnp.where(on, jnp.broadcast_to(named[e : e + 1, :], (ROWS, 256)), 0.0)
                sel_f[pl.ds(e * ROWS, ROWS), :] = one
                w_row = jnp.sum(one * weight[e : e + 1, :], axis=-1, keepdims=True)
                scale[hh, pl.ds(e * ROWS, ROWS), :] = jnp.broadcast_to(
                    jnp.where(c == 0, jnp.ones_like(w_row), w_row), (ROWS, 128)
                )
            sel[hh, :, :] = sel_f[...].astype(BF)

    def select(k):
        n = LANES[k]
        hs = [0, 1] if EARLY[k] else [h]
        for i, hh in enumerate(hs):
            for s in range(8):
                arrived(gath.at[k, hh, pl.ds(TOK * s, TOK), pl.ds(0, n)], xsem.at[k, i, s])
        if k + WINDOW < NK:
            send_x(k + WINDOW)
        for i, hh in enumerate(hs):
            picked = dot(sel[hh], gath[k, hh, :, 0:n])
            picked = (picked * scale[hh, :, 0:1]).astype(BF)
            flat(rows, k, hh)[:, 0:n] = picked
            ys = 2 * half + hh if EARLY[k] else y
            for dz in range(4):
                for pr in range(2):
                    zz, yy = z_peer(dz, pr)
                    pp = half + pr * (1 - 2 * half)
                    src = slabs(rows, (k, hh), (zz * 2 + pp) * ROWS, ROWS, n)
                    dst = slabs(xd, (k, c), ys * BLK + z * ROWS, ROWS, n)
                    sem = zsem.at[k, i, pr, z]
                    if dz == 0 and pr == 0:
                        pltpu.make_async_copy(src, dst, sem).start()
                    else:
                        put(src, dst, sem, device(x, zz, yy, c))

    def block(k, ys):
        return slabs(xd, (k, c), ys * BLK, BLK, LANES[k])

    def wait_z(k, i, pr, ys):
        n = LANES[k]
        for s in range(4):
            arrived(slabs(xd, (k, c), ys * BLK + s * ROWS, ROWS, n), zsem.at[k, i, pr, s])

    def to_core(k, ys):
        put(block(k, ys), block(k, ys), csem.at[k, ys], device(x, z, y, 1 - c))

    def forward(k):
        if EARLY[k]:
            for pr in range(2):
                for i in range(2):
                    ys = 2 * (half + pr * (1 - 2 * half)) + i
                    wait_z(k, i, pr, ys)
                    to_core(k, ys)
        else:
            for pr, ys in enumerate((y, yl)):
                wait_z(k, 0, pr, ys)
                put(block(k, ys), block(k, ys), ysem.at[k, pr], device(x, z, yp, c))
                to_core(k, ys)

    def finish(k):
        if not EARLY[k]:
            for pr, ys in enumerate((yp, 3 - yp)):
                arrived(block(k, ys), ysem.at[k, pr])
                to_core(k, ys)

    def up_matmuls(k):
        n, v, lo = LANES[k], VALID[k], k * CW
        for ys in range(4):
            arrived(slabs(xd, (k, 1 - c), ys * BLK, BLK, n), csem.at[k, ys])
        if k == 0:
            for w in weights:
                w.wait()
        xs = flat(xd, k, 0)[:, 0:v]
        gate = dot_t(xs, wg[:, lo : lo + v])
        gate_a[...] = gate if k == 0 else gate_a[...] + gate
        up = dot_t(xs, wu[:, lo : lo + v])
        up_a[...] = up if k == 0 else up_a[...] + up
        dhid = dot_t(flat(xd, k, 1)[:, 0:v], wd[:, lo : lo + v])
        dhid_a[...] = dhid if k == 0 else dhid_a[...] + dhid

    build()
    for step in range(NK + AHEAD[2]):
        if step < NK:
            select(step)
        for stage, after in zip((forward, finish, up_matmuls), AHEAD, strict=True):
            if 0 <= step - after < NK:
                stage(step - after)

    def pointwise(i, carry):
        b = pl.ds(pl.multiple_of(i * BLK, BLK), BLK)
        gate = gate_a[b, :]
        sig = jax.nn.sigmoid(alpha * gate)
        glu = gate * sig
        up1 = up_a[b, :] + 1.0
        gate_a[b, :] = glu * up1
        d_hid = dhid_a[b, :]
        du[b, :] = (d_hid * glu).astype(BF)
        dg[b, :] = (d_hid * up1 * (sig + alpha * gate * sig * (1.0 - sig))).astype(BF)
        return carry

    lax.fori_loop(0, 4, pointwise, 0)

    def partial(k):
        lo, v = k * CW, VALID[k]
        if v < CW:
            part[k, 1, :, :] = jnp.zeros((TOTAL, HW), BF)
        p = dot(dg[...], wg[:, lo : lo + v]) + dot(du[...], wu[:, lo : lo + v])
        p = p.astype(BF)
        part[k, 0, :, :] = p[:, 0:HW]
        part[k, 1, :, 0 : v - HW] = p[:, HW:v]
        put(part.at[k, 1 - c], part_got.at[k], rcsem.at[k], device(x, z, y, 1 - c))

    def back_z(k, src_ref, base_of):
        for pr in range(2):
            ydst = yl if pr else y
            his = [0, 1] if EARLY[k] else [0]
            for i in his:
                hd = i if EARLY[k] else lax.rem(ydst, 2)
                for dz in range(4):
                    zz = lax.rem(z + dz, 4)
                    src = slabs(src_ref, (k,), base_of(pr, i) * BLK + zz * ROWS, ROWS, HW)
                    dst = slabs(z_got, (k, hd), (z * 2 + half) * ROWS, ROWS, HW)
                    sem = rzsem.at[k, i, z * 2 + half]
                    if dz == 0 and pr == 0:
                        pltpu.make_async_copy(src, dst, sem).start()
                    else:
                        put(src, dst, sem, device(x, zz, ydst, c))

    def back_core(k):
        arrived(part_got.at[k], rcsem.at[k])
        flat(psum, k)[...] = (part[k, c].astype(F32) + part_got[k].astype(F32)).astype(BF)
        if EARLY[k]:
            back_z(k, psum, lambda pr, i: 2 * (half + pr * (1 - 2 * half)) + i)
        else:
            for j, ys in enumerate((yp, 3 - yp)):
                put(
                    slabs(psum, (k,), ys * BLK, BLK, HW), slabs(h_got, (k,), j * BLK, BLK, HW),
                    rhsem.at[k, j], device(x, z, yp, c),
                )

    def back_pair(k):
        if not EARLY[k]:
            for j, ys in enumerate((y, yl)):
                arrived(slabs(h_got, (k,), j * BLK, BLK, HW), rhsem.at[k, j])
                b = pl.ds(pl.multiple_of(ys * BLK, BLK), BLK)
                to = pl.ds(j * BLK, BLK)
                flat(drow, k)[to, :] = (
                    flat(psum, k)[b, :].astype(F32) + flat(h_got, k)[to, :].astype(F32)
                ).astype(BF)
            back_z(k, drow, lambda pr, i: pr)

    def back_token(k):
        hs = [0, 1] if EARLY[k] else [h]
        for i, hh in enumerate(hs):
            for e in range(8):
                arrived(slabs(z_got, (k, hh), e * ROWS, ROWS, HW), rzsem.at[k, i, e])
        for i, hh in enumerate(hs):
            tsum[k, hh, :, :] = dot_0(sel[hh], flat(z_got, k, hh)[...]).astype(BF)
            for p in peers_x:
                xx, cc = x_peer(*p)
                put(
                    tsum.at[k, hh, pl.ds((2 * xx + cc) * TOK, TOK), :],
                    x_got.at[k, hh, src_mine],
                    rxsem.at[k, i, src_mine],
                    device(xx, z, y, cc),
                )
            pltpu.make_async_copy(
                tsum.at[k, hh, pl.ds(src_mine * TOK, TOK), :],
                x_got.at[k, hh, src_mine],
                rxsem.at[k, i, src_mine],
            ).start()

    def gather_sum(k, hh, r):
        s = x_got[k, hh, r].astype(F32)
        for j in range(1, 4):
            s = s + x_got[k, hh, 2 * j + r].astype(F32)
        return s

    def back_x(k):
        hs = [0, 1] if EARLY[k] else [h]
        for i, hh in enumerate(hs):
            for s in range(8):
                arrived(x_got.at[k, hh, s], rxsem.at[k, i, s])
        for r in range(2):
            dn[2 * k + r] = gather_sum(k, h, r)
        if EARLY[k]:
            for r in range(2):
                f_out[k, r] = gather_sum(k, 1 - h, r).astype(BF)
            put(f_out.at[k], f_got.at[k], rfsem.at[k], device(x, z, yp, c))

    def back_last(k):
        if EARLY[k]:
            arrived(f_got.at[k], rfsem.at[k])
            for r in range(2):
                dn[2 * k + r] = dn[2 * k + r] + f_got[k, r].astype(F32)

    def grad(which, b):
        left = (dg_t, du_t, hid_t)[which]
        out = (wg, wu, wd)[which]
        for k in range(NK):
            lo, v = k * CW, VALID[k]
            out[b * GB : (b + 1) * GB, lo : lo + v] = dot(
                left[b * GB : (b + 1) * GB, :], flat(xd, k, which // 2)[:, 0:v]
            ).astype(BF)

    fill = [lambda w=w, b=b: grad(w, b) for w in (2, 0, 1) for b in range(NG)]

    for step in range(NK + BACK[-1]):
        if step < NK:
            partial(step)
        if step == 0:
            hid_t[...] = gate_a[...].T.astype(BF)
            dg_t[...] = dg[...].T
            du_t[...] = du[...].T
        for i, stage in enumerate((back_core, back_pair, back_token, back_x, back_last)):
            if 0 <= step - BACK[i] < NK:
                stage(step - BACK[i])
            if i == 1 and step >= 2 and (len(fill) > 2 * NG or step >= NK - 1) and fill:
                fill.pop(0)()
    while fill:
        fill.pop(0)()

    total = jnp.zeros((TOK, 1), F32)
    for k in range(NK):
        for r in range(2):
            lo = k * CW + r * HW
            v = max(0, min(HW, D - lo))
            if v:
                u = dn[2 * k + r, :, 0:v] * gain(lo, v)
                dn[2 * k + r, :, 0:v] = u
                total = total + jnp.sum(tf[:, lo : lo + v] * u, axis=-1, keepdims=True)
    mixed = rstd * rstd * rstd * (total / D)
    for k in range(NK):
        for r in range(2):
            lo = k * CW + r * HW
            v = max(0, min(HW, D - lo))
            if v:
                dtok_ref[:, lo : lo + v] = (
                    rstd * dn[2 * k + r, :, 0:v] - tf[:, lo : lo + v] * mixed
                ).astype(BF)

    for cp in sends:
        cp.wait_send()


def n_sends():
    early = sum(EARLY)
    late = NK - early
    n = early + (1 if early else 0)
    n += 7 * (late + 2 * early) + 7 * (2 if early else 1)
    n += 7 * (late + 2 * early) + 2 * late + 4 * NK
    n += NK + 2 * late + 7 * (late + 2 * early) + 7 * (late + 2 * early) + early
    return n


def write_out(t, a, b, c, t_hbm, a_hbm, b_hbm, c_hbm, sem):
    copies = [
        pltpu.make_async_copy(src, dst, sem.at[i])
        for i, (src, dst) in enumerate(((t, t_hbm), (a, a_hbm), (b, b_hbm), (c, c_hbm)))
    ]
    for cp in copies:
        cp.start()
    for cp in copies:
        cp.wait()


def local(tokens, norm_gain, expert_ids, combine_weight, cotangent, w_gate, w_up, w_down):
    vm = pl.BlockSpec(memory_space=pltpu.VMEM)
    hbm = pl.BlockSpec(memory_space=pl.ANY)
    dma = pltpu.SemaphoreType.DMA
    scratch = [
        pltpu.VMEM((TOK, D), BF), pltpu.VMEM((D,), F32), pltpu.VMEM((TOP, TOK), jnp.int32),
        pltpu.VMEM((TOP, TOK), F32), pltpu.VMEM((TOK, D), BF),
        pltpu.VMEM((NK, 2, 2, TOK, CW), BF),
        pltpu.VMEM((2, 8, 256), F32), pltpu.VMEM((2, 8, 8, 256), F32),
        pltpu.VMEM((NK, 2, 256, CW), BF),
        pltpu.VMEM((NK, 2, ROWS, 8, CW), BF),
        pltpu.VMEM((NK, 2, TOTAL // 8, 8, CW), BF),
        pltpu.VMEM((8 * ROWS, 256), F32), pltpu.VMEM((2, 8 * ROWS, 256), BF),
        pltpu.VMEM((2, 8 * ROWS, 128), F32),
        pltpu.VMEM((TOTAL, FQ), F32), pltpu.VMEM((TOTAL, FQ), F32), pltpu.VMEM((TOTAL, FQ), F32),
        pltpu.VMEM((TOTAL, FQ), BF), pltpu.VMEM((TOTAL, FQ), BF),
        pltpu.VMEM((FQ, TOTAL), BF), pltpu.VMEM((FQ, TOTAL), BF), pltpu.VMEM((FQ, TOTAL), BF),
        pltpu.VMEM((NK, 2, TOTAL, HW), BF),
        pltpu.VMEM((NK, TOTAL, HW), BF),
        pltpu.VMEM((NK, TOTAL // 8, 8, HW), BF),
        pltpu.VMEM((NK, BLK // 4, 8, HW), BF), pltpu.VMEM((NK, BLK // 4, 8, HW), BF),
        pltpu.VMEM((NK, 2, ROWS, 8, HW), BF), pltpu.VMEM((NK, 2, 256, HW), BF),
        pltpu.VMEM((NK, 2, 8, TOK, HW), BF),
        pltpu.VMEM((NK, 2, TOK, HW), BF), pltpu.VMEM((NK, 2, TOK, HW), BF),
        pltpu.VMEM((2 * NK, TOK, HW), F32),
        dma((3,)), dma((5,)), dma((2, 8)), dma((1,)), dma((NK + 1,)), dma((1,)), dma((NK, 2, 8)),
        dma((NK, 2, 2, 4)), dma((NK, 2)), dma((NK, 4)), dma((NK,)), dma((NK, 2)), dma((NK, 2, 8)),
        dma((NK, 2, 8)), dma((NK,)), dma((n_sends(),)),
    ]
    d_tokens, grad_gate, grad_up, grad_down = pl.pallas_call(
        kernel,
        out_shape=(
            pltpu.VMEM((TOK, D), BF),
            pltpu.VMEM((1, FQ, D), BF),
            pltpu.VMEM((1, FQ, D), BF),
            pltpu.VMEM((1, FQ, D), BF),
        ),
        in_specs=[hbm] * 8,
        out_specs=(vm, vm, vm, vm),
        scratch_shapes=scratch,
        compiler_params=pltpu.CompilerParams(
            collective_id=0, has_side_effects=True, vmem_limit_bytes=48 << 20
        ),
    )(
        tokens, norm_gain, expert_ids.T, combine_weight.T, cotangent,
        jnp.swapaxes(w_gate, 1, 2), jnp.swapaxes(w_up, 1, 2), w_down,
    )
    d_tokens, grad_gate, grad_up, grad_down = pl.pallas_call(
        write_out,
        out_shape=(jax.ShapeDtypeStruct((TOK, D), BF),)
        + (jax.ShapeDtypeStruct((1, FQ, D), BF),) * 3,
        in_specs=[vm] * 4,
        out_specs=(hbm,) * 4,
        scratch_shapes=[dma((4,))],
        compiler_params=pltpu.CompilerParams(has_side_effects=True, vmem_limit_bytes=1 << 20),
    )(d_tokens, grad_gate, grad_up, grad_down)
    return d_tokens, jnp.swapaxes(grad_gate, 1, 2), jnp.swapaxes(grad_up, 1, 2), grad_down


def solution(mesh):
    placed = (
        P("sq", None),
        P(),
        P("sq", None),
        P("sq", None),
        P("sq", None),
        P("sq", None, None),
        P("sq", None, None),
        P("sq", None, None),
    )
    return jax.shard_map(
        local,
        mesh=mesh,
        in_specs=placed,
        out_specs=(P("sq", None), P("sq", None, None), P("sq", None, None), P("sq", None, None)),
        check_vma=False,
    )
```
